256 devices in a mesh: row: 16 (over z, y_hi), col: 16 (over y_lo, x, core).
Axes of the slice: x: 4, y: 4 (y_hi: 2, y_lo: 2; y = y_hi * 2 + y_lo), z: 8, core: 2. Of those that a mesh axis runs over, the one named last changes fastest.
Arguments:
- tokens: bfloat16 [1, 256, 256, 512], P(None, 'row', 'col'), may hold values from -6 to 6
- cotangent: bfloat16 [1, 256, 256, 512], P(None, 'row', 'col'), may hold values from -16 to 16
- regions: int32 [1, 256, 256], P(None, 'row', 'col'), may hold values from 0 to 3
- qkv_weight: bfloat16 [512, 1536], replicated, may hold values from -0.25 to 0.25
- query_bias: float32 [512], replicated, may hold values from -3 to 3
- value_bias: float32 [512], replicated, may hold values from -3 to 3
- logit_scale: float32 [16], replicated, may hold values from 1.5 to 5.3
- bias_network_entry_weight: float32 [2, 512], replicated, may hold values from -4 to 4
- bias_network_entry_bias: float32 [512], replicated, may hold values from -3 to 3
- bias_network_exit_weight: float32 [512, 16], replicated, may hold values from -0.25 to 0.25
- proj_weight: bfloat16 [512, 512], replicated, may hold values from -0.25 to 0.25
- proj_bias: float32 [512], replicated, may hold values from -3 to 3
- attn_gain: float32 [512], replicated, may hold values from 0.5 to 1.5
- attn_shift: float32 [512], replicated, may hold values from -3 to 3
- hidden_weight: bfloat16 [512, 2048], replicated, may hold values from -0.25 to 0.25
- hidden_bias: float32 [2048], replicated, may hold values from -3 to 3
- output_weight: bfloat16 [2048, 512], replicated, may hold values from -0.125 to 0.125
- output_bias: float32 [512], replicated, may hold values from -3 to 3
- mlp_gain: float32 [512], replicated, may hold values from 0.5 to 1.5
Outputs:
- grad_tokens: bfloat16 [1, 256, 256, 512], P(None, 'row', 'col')
- gradient_query_key_value: float32 [786432], P(('row', 'col'))
- grad_proj: float32 [262144], P(('row', 'col'))
- grad_hidden: float32 [1048576], P(('row', 'col'))
- grad_output: float32 [1048576], P(('row', 'col'))
- grad_vectors: float32 [8, 512], replicated
- grad_hidden_bias: float32 [2048], replicated
- grad_logit_scale: float32 [16], replicated
- grad_bias_mlp_in: float32 [3, 512], replicated
- grad_bias_mlp_out: float32 [512, 16], replicated
The draws below stay inside these ranges and needn't reach their ends.
All inputs are finite; a program needn't handle non-finite values.
Results may differ from the reference program's by a relative error of at most 0.015.
The reference program's roundings to bfloat16 on the way count: a program that leaves them out, or rounds other values in their place, can miss the bound.
Values may be sent and summed in bfloat16 or wider, within the bound.
No kernel may reach another device: no remote copies, remote signals or barrier semaphores. Data moves between devices by JAX's collectives and lax.ppermute only.
A program may use at most 256 MiB of HBM per device.

```python
import math
import jax
import jax.numpy as jnp
from jax import lax

D = 512
HEAD_TOTAL = 16
FF = 2048
POSITION_UNITS = 512
WIN = 16
SHIFT = 8
BATCH = 1
GH = 256
GW = 256
TOKENS = 65536


def draw_cotangent(key, part):
    key = jax.random.fold_in(key, 11)
    row_pos = jnp.arange(GH).astype(jnp.float32) / max(GH - 1, 1)
    base = jax.random.truncated_normal(key, -4.0, 4.0, (BATCH, GH, GW, D), jnp.float32)
    factor = (1.0 + 2.0 * row_pos)[None, :, None, None] * jnp.ones((1, 1, GW, 1), jnp.float32)
    return (base * factor).astype(jnp.bfloat16)


def set_ends(drawn, stream_key, least, top_value):
    longest = drawn.shape.index(max(drawn.shape))
    spots = []
    for shift in (0, 1):
        where = [jax.random.randint(jax.random.fold_in(stream_key, axis), (), 0, length) for axis, length in enumerate(drawn.shape)]
        where[longest] = (where[longest] + shift) % drawn.shape[longest]
        spots.append(tuple(where))
    return drawn.at[spots[0]].set(least).at[spots[1]].set(top_value)


def shard_levels(stream_key, dims, pieces, least, top_value):
    level, own = 1.0, jax.random.fold_in(stream_key, 6)
    for dim, blocks in pieces:
        draws = jnp.exp(jax.random.uniform(jax.random.fold_in(own, dim), (blocks,), jnp.float32, least / len(pieces), top_value / len(pieces)))
        level = level * jnp.repeat(draws, dims[dim] // blocks).reshape([-1 if axis == dim else 1 for axis in range(len(dims))])
    return level


def noise(own_key, dims, width, bound, shards=(), held_as=jnp.bfloat16):
    result = width * jax.random.normal(own_key, dims, jnp.float32)
    if shards:
        result = result * shard_levels(own_key, dims, shards, -0.22, 0.18)
    return jnp.clip(result, -bound, bound).astype(held_as)


def setup_inputs(seed: int = 0) -> dict:
    splits = jax.random.split(jax.random.key(seed), 20)
    return {
        "tokens": noise(splits[0], (BATCH, GH, GW, D), 1.0, 6.0, ((1, 16), (2, 16))),
        "cotangent": draw_cotangent(jax.random.fold_in(splits[19], 71), 0),
        "regions": set_ends(jax.random.randint(splits[2], (BATCH, GH, GW), 0, 4), jax.random.fold_in(splits[2], 1), 0, 3).astype(jnp.int32),
        "qkv_weight": noise(splits[3], (D, 3 * D), D ** -0.5, 0.25),
        "query_bias": noise(splits[4], (D,), 0.5, 3.0, (), jnp.float32),
        "value_bias": noise(splits[5], (D,), 0.5, 3.0, (), jnp.float32),
        "logit_scale": jnp.clip(jax.random.uniform(splits[6], (HEAD_TOTAL,), jnp.float32, 1.5, 5.3), 1.5, 5.3),
        "bias_network_entry_weight": noise(splits[7], (2, POSITION_UNITS), 2 ** -0.5, 4.0, (), jnp.float32),
        "bias_network_entry_bias": noise(splits[8], (POSITION_UNITS,), 0.5, 3.0, (), jnp.float32),
        "bias_network_exit_weight": noise(splits[9], (POSITION_UNITS, HEAD_TOTAL), POSITION_UNITS ** -0.5, 0.25, (), jnp.float32),
        "proj_weight": noise(splits[10], (D, D), D ** -0.5, 0.25),
        "proj_bias": noise(splits[11], (D,), 0.5, 3.0, (), jnp.float32),
        "attn_gain": jnp.clip(1.0 + 0.1 * jax.random.normal(splits[12], (D,), jnp.float32), 0.5, 1.5),
        "attn_shift": noise(splits[13], (D,), 0.5, 3.0, (), jnp.float32),
        "hidden_weight": noise(splits[14], (D, FF), D ** -0.5, 0.25),
        "hidden_bias": noise(splits[15], (FF,), 0.5, 3.0, (), jnp.float32),
        "output_weight": noise(splits[16], (FF, D), FF ** -0.5, 0.125),
        "output_bias": noise(splits[17], (D,), 0.5, 3.0, (), jnp.float32),
        "mlp_gain": jnp.clip(1.0 + 0.1 * jax.random.normal(splits[18], (D,), jnp.float32), 0.5, 1.5),
    }


top_precision = lax.Precision.HIGHEST
log_cap = math.log(100.0)

def batched(form, former, latter):
    return jnp.einsum(form, former.astype(jnp.float32), latter.astype(jnp.float32))

def layer_stats(inputs, scale_vector, shift_vector):
    center = inputs - lax.optimization_barrier(jnp.mean(inputs, -1, keepdims=True))
    inverse = lax.rsqrt(lax.optimization_barrier(jnp.mean(center * center, -1, keepdims=True)) + 1e-05)
    normed = center * inverse
    return (normed * scale_vector + shift_vector, normed, inverse)

def layer_back(upstream, normed, inverse, scale_vector):
    scaled = upstream * scale_vector
    inner = scaled - lax.optimization_barrier(jnp.mean(scaled, -1, keepdims=True)) - normed * lax.optimization_barrier(jnp.mean(scaled * normed, -1, keepdims=True))
    return (inverse * inner, lax.optimization_barrier(jnp.sum(upstream * normed, 0)), lax.optimization_barrier(jnp.sum(upstream, 0)))

def gelu_parts(inputs):
    cumulative = 0.5 * (1.0 + jax.scipy.special.erf(inputs / math.sqrt(2.0)))
    density = jnp.exp(-0.5 * inputs * inputs) / math.sqrt(2.0 * math.pi)
    return (inputs * cumulative, cumulative + inputs * density)

def relative_onehot(side):
    first_idx = jnp.arange(side)[:, None, None]
    second_idx = jnp.arange(side)[None, :, None]
    target = jnp.arange(2 * side - 1)[None, None, :]
    return jnp.where(first_idx - second_idx + side - 1 == target, 1.0, 0.0).astype(jnp.float32)

def position_coords(side):
    offsets = jnp.arange(2 * side - 1).astype(jnp.float32) - (side - 1)
    scaled = offsets / (side - 1) * 8.0
    logged = jnp.sign(scaled) * jnp.log2(jnp.abs(scaled) + 1.0) / 3.0
    return jnp.stack([jnp.repeat(logged, 2 * side - 1), jnp.tile(logged, 2 * side - 1)], 1)

def position_table(side, mlp_in, mlp_mid, mlp_out):
    coords = position_coords(side)
    before = jnp.dot(coords, mlp_in, precision=top_precision) + mlp_mid
    hidden = jnp.maximum(before, 0.0)
    squashed = jax.nn.sigmoid(jnp.dot(hidden, mlp_out, precision=top_precision))
    return (coords, before, hidden, squashed)

def full_bias(squashed, side):
    rel_span = 2 * side - 1
    table_grid = 16.0 * squashed.T.reshape(-1, rel_span, rel_span)
    onehot = relative_onehot(side)
    spread = jnp.einsum('ijc,abd,hcd->hiajb', onehot, onehot, table_grid, precision=top_precision)
    return spread.reshape(table_grid.shape[0], side * side, side * side)

def table_grad(bias_sum, squashed, side):
    rel_span = 2 * side - 1
    head_count = bias_sum.shape[0]
    onehot = relative_onehot(side)
    folded = jnp.einsum('hiajb,ijc,abd->hcd', bias_sum.reshape(head_count, side, side, side, side), onehot, onehot, precision=top_precision)
    return folded.reshape(head_count, rel_span * rel_span).T * 16.0 * squashed * (1.0 - squashed)

def mlp_back(table_flat, coords, before, hidden, mlp_out):
    grad_out = jnp.dot(hidden.T, table_flat, precision=top_precision)
    grad_pos = jnp.where(before > 0.0, jnp.dot(table_flat, mlp_out.T, precision=top_precision), 0.0)
    grad_in = jnp.dot(coords.T, grad_pos, precision=top_precision)
    return (jnp.concatenate([grad_in, lax.optimization_barrier(jnp.sum(grad_pos, 0))[None]], 0), grad_out)

def window_grads(windows, upstream, regions, bias_full, weights):
    qkv_weight, query_bias, value_bias, logit_scale, proj_weight, proj_bias, attn_gain, attn_shift, hidden_weight, hidden_bias, output_weight, output_bias, mlp_gain = weights
    amount, length, breadth = windows.shape
    head_count = logit_scale.shape[0]
    head_size = breadth // head_count
    rows_all = amount * length
    flat_tokens = windows.reshape(rows_all, breadth)
    projected_qkv = jnp.dot(flat_tokens, qkv_weight, preferred_element_type=jnp.float32)
    queries = (projected_qkv[:, :breadth] + query_bias).reshape(amount, length, head_count, head_size)
    key_raw = projected_qkv[:, breadth:2 * breadth].reshape(amount, length, head_count, head_size)
    values = (projected_qkv[:, 2 * breadth:] + value_bias).reshape(amount, length, head_count, head_size).astype(jnp.bfloat16)
    query_inverse = lax.rsqrt(lax.optimization_barrier(jnp.sum(queries * queries, -1, keepdims=True)) + 1e-06)
    key_inverse = lax.rsqrt(lax.optimization_barrier(jnp.sum(key_raw * key_raw, -1, keepdims=True)) + 1e-06)
    query_unit = queries * query_inverse
    key_unit = key_raw * key_inverse
    query_low = query_unit.astype(jnp.bfloat16)
    key_low = key_unit.astype(jnp.bfloat16)
    cosine = batched('wihe,wjhe->whij', query_low, key_low)
    scales = jnp.exp(jnp.minimum(logit_scale, log_cap))[None, :, None, None]
    allowed = (regions[:, :, None] == regions[:, None, :])[:, None]
    attention_logits = jnp.where(allowed, scales * cosine + bias_full[None], -1000000000.0)
    highest = lax.optimization_barrier(jnp.max(attention_logits, -1, keepdims=True))
    powers = jnp.exp(attention_logits - highest)
    probs = powers / lax.optimization_barrier(jnp.sum(powers, -1, keepdims=True))
    probs_low = probs.astype(jnp.bfloat16)
    attended = batched('whij,wjhe->wihe', probs_low, values).astype(jnp.bfloat16).reshape(rows_all, breadth)
    projected = jnp.dot(attended, proj_weight, preferred_element_type=jnp.float32) + proj_bias
    attn_out, attn_normed, attn_inverse = layer_stats(projected, attn_gain, attn_shift)
    middle = flat_tokens.astype(jnp.float32) + attn_out
    middle_low = middle.astype(jnp.bfloat16)
    before_act = jnp.dot(middle_low, hidden_weight, preferred_element_type=jnp.float32) + hidden_bias
    activated, slope = gelu_parts(before_act)
    activated_low = activated.astype(jnp.bfloat16)
    emitted = jnp.dot(activated_low, output_weight, preferred_element_type=jnp.float32) + output_bias
    unused_out, mlp_normed, mlp_inverse = layer_stats(emitted, mlp_gain, 0.0)
    incoming = upstream.reshape(rows_all, breadth).astype(jnp.float32)
    grad_emitted, grad_mlp_gain, grad_mlp_shift = layer_back(incoming, mlp_normed, mlp_inverse, mlp_gain)
    emitted_low = grad_emitted.astype(jnp.bfloat16)
    grad_output = jnp.dot(activated_low.T, emitted_low, preferred_element_type=jnp.float32)
    grad_act = jnp.dot(emitted_low, output_weight.T, preferred_element_type=jnp.float32)
    grad_before = grad_act * slope
    before_low = grad_before.astype(jnp.bfloat16)
    grad_hidden = jnp.dot(middle_low.T, before_low, preferred_element_type=jnp.float32)
    grad_middle = incoming + jnp.dot(before_low, hidden_weight.T, preferred_element_type=jnp.float32)
    grad_projected, grad_attn_gain, grad_attn_shift = layer_back(grad_middle, attn_normed, attn_inverse, attn_gain)
    projected_low = grad_projected.astype(jnp.bfloat16)
    grad_proj = jnp.dot(attended.T, projected_low, preferred_element_type=jnp.float32)
    grad_attended = jnp.dot(projected_low, proj_weight.T, preferred_element_type=jnp.float32).astype(jnp.bfloat16)
    grad_attended = grad_attended.reshape(amount, length, head_count, head_size)
    grad_probs = batched('wihe,wjhe->whij', grad_attended, values)
    grad_values = batched('whij,wihe->wjhe', probs_low, grad_attended)
    grad_scores = probs * (grad_probs - lax.optimization_barrier(jnp.sum(probs * grad_probs, -1, keepdims=True)))
    grad_scale = lax.optimization_barrier(jnp.sum(grad_scores * cosine, (0, 2, 3)))
    grad_logit = jnp.where(logit_scale < log_cap, grad_scale * scales[0, :, 0, 0], 0.0)
    grad_bias = lax.optimization_barrier(jnp.sum(grad_scores, 0))
    grad_cosine = (grad_scores * scales).astype(jnp.bfloat16)
    grad_qunit = batched('whij,wjhe->wihe', grad_cosine, key_low)
    grad_kunit = batched('whij,wihe->wjhe', grad_cosine, query_low)
    grad_queries = query_inverse * (grad_qunit - query_unit * lax.optimization_barrier(jnp.sum(query_unit * grad_qunit, -1, keepdims=True)))
    grad_keys = key_inverse * (grad_kunit - key_unit * lax.optimization_barrier(jnp.sum(key_unit * grad_kunit, -1, keepdims=True)))
    grad_queries = grad_queries.reshape(rows_all, breadth)
    grad_values = grad_values.reshape(rows_all, breadth)
    grad_mixed = jnp.concatenate([grad_queries, grad_keys.reshape(rows_all, breadth), grad_values], 1).astype(jnp.bfloat16)
    gradient_query_key_value = jnp.dot(flat_tokens.T, grad_mixed, preferred_element_type=jnp.float32)
    grad_windows = (grad_middle + jnp.dot(grad_mixed, qkv_weight.T, preferred_element_type=jnp.float32)).astype(jnp.bfloat16)
    token_vectors = jnp.stack([lax.optimization_barrier(jnp.sum(grad_queries, 0)), lax.optimization_barrier(jnp.sum(grad_values, 0)), lax.optimization_barrier(jnp.sum(grad_projected, 0)), grad_attn_gain, grad_attn_shift, lax.optimization_barrier(jnp.sum(grad_emitted, 0)), grad_mlp_gain, grad_mlp_shift])
    matrices = (gradient_query_key_value, grad_proj, grad_hidden, grad_output)
    return (grad_windows.reshape(amount, length, breadth), matrices, token_vectors, lax.optimization_barrier(jnp.sum(grad_before, 0)), grad_logit, grad_bias)

def to_windows(field):
    images, height, across, channels = field.shape
    parts = field.reshape(images, height // WIN, WIN, across // WIN, WIN, channels).transpose(0, 1, 3, 2, 4, 5)
    return parts.reshape(-1, WIN * WIN, channels)

def from_windows(windows, images, height, across):
    channels = windows.shape[-1]
    parts = windows.reshape(images, height // WIN, across // WIN, WIN, WIN, channels).transpose(0, 1, 3, 2, 4, 5)
    return parts.reshape(images, height, across, channels)

def reference(tokens, cotangent, regions, qkv_weight, query_bias, value_bias, logit_scale, bias_network_entry_weight, bias_network_entry_bias, bias_network_exit_weight, proj_weight, proj_bias, attn_gain, attn_shift, hidden_weight, hidden_bias, output_weight, output_bias, mlp_gain):
    weights = (qkv_weight, query_bias, value_bias, logit_scale, proj_weight, proj_bias, attn_gain, attn_shift, hidden_weight, hidden_bias, output_weight, output_bias, mlp_gain)
    coords, before, hidden, squashed = position_table(WIN, bias_network_entry_weight, bias_network_entry_bias, bias_network_exit_weight)
    bias_full = full_bias(squashed, WIN)
    shifted = to_windows(jnp.roll(tokens, (-SHIFT, -SHIFT), (1, 2)))
    upstream = to_windows(jnp.roll(cotangent, (-SHIFT, -SHIFT), (1, 2)))
    region_windows = to_windows(regions[..., None])[..., 0]
    breadth = tokens.shape[3]
    zero_totals = (tuple((jnp.zeros(w.shape, jnp.float32) for w in (qkv_weight, proj_weight, hidden_weight, output_weight))), jnp.zeros((8, breadth), jnp.float32), jnp.zeros(hidden_bias.shape, jnp.float32), jnp.zeros(logit_scale.shape, jnp.float32), jnp.zeros(bias_full.shape, jnp.float32))

    def scan_step(totals, window_item):
        window_piece, upstream_piece, region_piece = window_item
        grad_window, matrices, token_vectors, hidden_sum, logit_grad, bias_grad = window_grads(window_piece[None], upstream_piece[None], region_piece[None], bias_full, weights)
        added = jax.tree.map(lambda a, b: a + b, totals, (matrices, token_vectors, hidden_sum, logit_grad, bias_grad))
        return (added, grad_window[0])
    totals, grad_windows = lax.scan(scan_step, zero_totals, (shifted, upstream, region_windows))
    matrices, token_vectors, hidden_sum, logit_grad, bias_sum = totals
    grad_tokens = jnp.roll(from_windows(grad_windows, BATCH, GH, GW), (SHIFT, SHIFT), (1, 2))
    grad_factor = 1.0 / math.sqrt(TOKENS)
    folded = table_grad(bias_sum, squashed, WIN) * grad_factor
    mlp_first, mlp_second = mlp_back(folded, coords, before, hidden, bias_network_exit_weight)
    return (grad_tokens, (matrices[0] * grad_factor).reshape(-1), (matrices[1] * grad_factor).reshape(-1), (matrices[2] * grad_factor).reshape(-1), (matrices[3] * grad_factor).reshape(-1), token_vectors * grad_factor, hidden_sum * grad_factor, logit_grad * grad_factor, mlp_first, mlp_second)
```

```python
import math

import jax
import jax.numpy as jnp
from jax import lax
from jax.experimental import pallas as pl
from jax.experimental.pallas import tpu as pltpu
from jax.sharding import Mesh
from jax.sharding import PartitionSpec as P

WIN = 16
HALF = 8
T = 256
D = 512
HEADS = 16
E = 32
FF = 2048
CH = 512
LANES = 512
ALL = ("z", "yh", "yl", "x", "core")
AXES = (("z", 8), ("yh", 2), ("yl", 2), ("x", 4), ("core", 2))
DEVICES = 256
FACTOR = 1.0 / 256.0
LOG_CAP = math.log(100.0)
TOP = lax.Precision.HIGHEST
BF = jnp.bfloat16
F4 = jnp.float32
PARAMS = pltpu.CompilerParams(vmem_limit_bytes=56 * 1024 * 1024)


def dot(a, b, ca, cb, precision=None):
    return lax.dot_general(
        a, b, (((ca,), (cb,)), ((), ())), precision=precision, preferred_element_type=F4
    )


def layer_stats(inputs):
    center = inputs - jnp.mean(inputs, -1, keepdims=True)
    inverse = lax.rsqrt(jnp.mean(center * center, -1, keepdims=True) + 1e-05)
    return center * inverse, inverse


def layer_back(upstream, normed, inverse, gain):
    scaled = upstream * gain
    inner = (
        scaled
        - jnp.mean(scaled, -1, keepdims=True)
        - normed * jnp.mean(scaled * normed, -1, keepdims=True)
    )
    return inverse * inner


def col_sum(block):
    return jnp.sum(block, 0, keepdims=True)


def offset_coords():
    lane = lax.broadcasted_iota(jnp.int32, (8, 2 * LANES), 1)
    parity = lane // LANES
    rest = lane - parity * LANES
    pair = rest // 32
    first = 2 * pair + parity
    second = rest - pair * 32
    valid = (first < 31) & (second < 31)

    def logged(index):
        u = (index.astype(F4) - 15.0) / 15.0 * 8.0
        size = jnp.log2(jnp.abs(u) + 1.0) / 3.0
        return jnp.where(u > 0.0, size, jnp.where(u < 0.0, -size, 0.0))

    row = lax.broadcasted_iota(jnp.int32, (8, 2 * LANES), 0)
    coords = jnp.where(
        row == 0, logged(first), jnp.where(row == 1, logged(second), jnp.where(row == 2, 1.0, 0.0))
    )
    return coords, valid


def low_half(shape):
    lane = lax.broadcasted_iota(jnp.int32, shape, len(shape) - 1)
    return lane % 32 < 16


def stack_rows(entry, bias):
    return jnp.concatenate([entry, bias, jnp.zeros((5, entry.shape[1]), F4)], 0)


def bias_kernel(entry_ref, mid_ref, exit_ref, wide_ref, squashed_ref, before_ref, scratch):
    coords, _ = offset_coords()
    before = dot(stack_rows(entry_ref[...], mid_ref[...]), coords, 0, 0, TOP)
    before_ref[...] = before
    hidden = jnp.maximum(before, 0.0)
    squashed = jax.nn.sigmoid(dot(exit_ref[...], hidden, 0, 0, TOP))
    squashed_ref[...] = squashed
    table = 16.0 * squashed
    even, odd = table[:, :LANES], table[:, LANES:]
    low = low_half((HEADS, LANES))
    for c in range(WIN):
        scratch[c] = jnp.where(
            low,
            pltpu.roll(even, (c - 15) % LANES, 1),
            pltpu.roll(odd, (c + 1) % LANES, 1),
        )
    for h in range(HEADS):
        wide_ref[h] = scratch[:, h, :]


def forward_kernel(
    own_ref, down_ref, right_ref, diag_ref, regions_ref, wide_ref,
    qkv_ref, qbias_ref, vbias_ref, logit_ref,
    proj_ref, pbias_ref, again_ref, ashift_ref,
    hidden_ref, hbias_ref, output_ref, obias_ref, mgain_ref,
    x_ref, probs_ref, qunit_ref, kunit_ref, inverse_ref, value_ref, att_ref,
    normed_ref, ainverse_ref, gmiddle_ref, vectors_ref, hsum_ref, ghidden_ref, goutput_ref,
    qlow_s, klow_s, act_s, slope_s,
):
    def assemble(i):
        top = jnp.concatenate([own_ref[i, HALF:, HALF:], right_ref[i]], 1)
        bottom = jnp.concatenate([down_ref[i], diag_ref[i]], 1)
        return jnp.concatenate([top, bottom], 0).reshape(T, D)

    x = assemble(0)
    x_ref[...] = x
    mixed = dot(x, qkv_ref[...], 1, 0)
    q = (mixed[:, :D] + qbias_ref[...]).T
    k = mixed[:, D : 2 * D].T
    value_ref[...] = (mixed[:, 2 * D :] + vbias_ref[...]).T.astype(BF)
    for index, (raw, unit_ref, low_s) in enumerate(
        ((q, qunit_ref, qlow_s), (k, kunit_ref, klow_s))
    ):
        split = raw.reshape(HEADS, E, T)
        inverse = lax.rsqrt(jnp.sum(split * split, 1, keepdims=True) + 1e-06)
        inverse_ref[index] = inverse
        unit = (split * inverse).reshape(D, T)
        unit_ref[...] = unit
        low_s[...] = unit.astype(BF)
    region_row = regions_ref[...]
    region_col = jnp.broadcast_to(region_row.astype(F4), (8, T)).T[:, :1]
    allowed = region_col == region_row.astype(F4)

    def head(h, carry):
        at = pl.ds(pl.multiple_of(h * E, E), E)
        scale = jnp.exp(jnp.minimum(jnp.full((1, T), logit_ref[h], F4), LOG_CAP))
        cosine = dot(klow_s[at, :], qlow_s[at, :], 0, 0)
        wide = wide_ref[h]
        rolled = [wide] + [pltpu.roll(wide, LANES - 16 * p, 1) for p in range(1, 8)]
        bias = jnp.concatenate(
            [
                rolled[(15 - r) % 8][:, (15 - r) // 8 * 128 : (15 - r) // 8 * 128 + T]
                for r in range(WIN)
            ],
            0,
        )
        logits = jnp.where(allowed, scale * cosine + bias, -1000000000.0)
        powers = jnp.exp(logits - jnp.max(logits, 0, keepdims=True))
        probs = powers / jnp.sum(powers, 0, keepdims=True)
        probs_ref[h] = probs
        att_ref[at, :] = dot(value_ref[at, :], probs.astype(BF), 1, 0).astype(BF)
        return carry

    lax.fori_loop(0, HEADS, head, 0, unroll=2)

    projected = dot(att_ref[...], proj_ref[...], 0, 0) + pbias_ref[...]
    attn_normed, attn_inverse = layer_stats(projected)
    normed_ref[...] = attn_normed
    ainverse_ref[...] = attn_inverse
    middle = x.astype(F4) + (attn_normed * again_ref[...] + ashift_ref[...])
    middle_low = middle.astype(BF)
    emitted = jnp.zeros((T, D), F4)
    for c in range(0, FF, CH):
        cut = slice(c, c + CH)
        before = dot(middle_low, hidden_ref[:, cut], 1, 0) + hbias_ref[:, cut]
        cumulative = 0.5 * (1.0 + lax.erf(before * (1.0 / math.sqrt(2.0))))
        density = jnp.exp(-0.5 * before * before) * (1.0 / math.sqrt(2.0 * math.pi))
        slope_s[:, cut] = cumulative + before * density
        act = (before * cumulative).astype(BF)
        act_s[:, cut] = act
        emitted += dot(act, output_ref[cut, :], 1, 0)
    normed, inverse = layer_stats(emitted + obias_ref[...])
    incoming = assemble(1).astype(F4)
    grad_emitted = layer_back(incoming, normed, inverse, mgain_ref[...])
    emitted_low = grad_emitted.astype(BF)
    vectors_ref[0:1, :] = col_sum(grad_emitted) * FACTOR
    vectors_ref[1:2, :] = col_sum(incoming * normed) * FACTOR
    vectors_ref[2:3, :] = col_sum(incoming) * FACTOR
    grad_middle = incoming
    for c in range(0, FF, CH):
        cut = slice(c, c + CH)
        grad_act = dot(emitted_low, output_ref[cut, :], 1, 1)
        grad_before = grad_act * slope_s[:, cut]
        hsum_ref[:, cut] = col_sum(grad_before) * FACTOR
        before_low = grad_before.astype(BF)
        goutput_ref[cut, :] = (dot(act_s[:, cut], emitted_low, 0, 0) * FACTOR).astype(BF)
        ghidden_ref[:, cut] = (dot(middle_low, before_low, 0, 0) * FACTOR).astype(BF)
        grad_middle += dot(before_low, hidden_ref[:, cut], 1, 1)
    gmiddle_ref[...] = grad_middle


def backward_kernel(
    x_ref, probs_ref, qunit_ref, kunit_ref, inverse_ref, value_ref, att_ref,
    normed_ref, ainverse_ref, gmiddle_ref, qkv_ref, logit_ref, proj_ref, again_ref,
    entry_ref, exit_ref, squashed_ref, before_ref,
    gqkv_ref, gproj_ref, own_ref, down_ref, right_ref, diag_ref,
    vectors_ref, glogit_ref, gentry_ref, gexit_ref,
    qlow_s, klow_s, gatt_s, gmixed_s, wide_s,
):
    grad_middle = gmiddle_ref[...]
    attn_normed = normed_ref[...]
    grad_projected = layer_back(grad_middle, attn_normed, ainverse_ref[...], again_ref[...])
    projected_low = grad_projected.astype(BF)
    vectors_ref[2:3, :] = col_sum(grad_projected) * FACTOR
    vectors_ref[3:4, :] = col_sum(grad_middle * attn_normed) * FACTOR
    vectors_ref[4:5, :] = col_sum(grad_middle) * FACTOR
    gproj_ref[...] = (dot(att_ref[...], projected_low, 1, 0) * FACTOR).astype(BF)
    gatt_s[...] = dot(proj_ref[...], projected_low, 1, 1).astype(BF)
    qlow_s[...] = qunit_ref[...].astype(BF)
    klow_s[...] = kunit_ref[...].astype(BF)

    def head(h, carry):
        at = pl.ds(pl.multiple_of(h * E, E), E)
        kat = pl.ds(pl.multiple_of(h * E + D, E), E)
        vat = pl.ds(pl.multiple_of(h * E + 2 * D, E), E)
        scale = jnp.exp(jnp.minimum(jnp.full((1, T), logit_ref[h], F4), LOG_CAP))
        qlow, klow, gatt = qlow_s[at, :], klow_s[at, :], gatt_s[at, :]
        probs = probs_ref[h]
        grad_probs = dot(value_ref[at, :], gatt, 0, 0)
        gmixed_s[vat, :] = dot(gatt, probs.astype(BF), 1, 1)
        grad_scores = probs * (grad_probs - jnp.sum(probs * grad_probs, 0, keepdims=True))
        cosine = dot(klow, qlow, 0, 0)
        live = jnp.full((1, T), logit_ref[h], F4) < LOG_CAP
        total = jnp.sum(jnp.sum(grad_scores * cosine, 0, keepdims=True), 1, keepdims=True)
        glogit_ref[pl.ds(h, 1), :] = jnp.where(live, total * scale * FACTOR, 0.0)[:, :128]
        grad_cosine = (grad_scores * scale).astype(BF)
        for index, (part, unit_ref, where) in enumerate(
            (
                (dot(klow, grad_cosine, 1, 0), qunit_ref, at),
                (dot(qlow, grad_cosine, 1, 1), kunit_ref, kat),
            )
        ):
            unit = unit_ref[at, :]
            gmixed_s[where, :] = inverse_ref[index, h] * (
                part - unit * jnp.sum(unit * part, 0, keepdims=True)
            )
        wide = None
        for p in range(8):
            first = grad_scores[(15 - p) * 16 : (16 - p) * 16]
            second = grad_scores[(7 - p) * 16 : (8 - p) * 16]
            blank = jnp.zeros((WIN, 128), F4)
            placed = jnp.concatenate(
                [first[:, :128], first[:, 128:] + second[:, :128], second[:, 128:], blank], 1
            )
            if p:
                placed = pltpu.roll(placed, 16 * p, 1)
            wide = placed if wide is None else wide + placed
        wide_s[h] = wide
        return carry

    lax.fori_loop(0, HEADS, head, 0, unroll=2)

    ones = jnp.ones((8, T), F4)
    vectors_ref[0:1, :] = dot(ones, gmixed_s[0:D, :], 1, 1, TOP)[:1] * FACTOR
    vectors_ref[1:2, :] = dot(ones, gmixed_s[2 * D :, :], 1, 1, TOP)[:1] * FACTOR
    vectors_ref[5:8, :] = jnp.zeros((3, D), F4)
    mixed = gmixed_s[...].astype(BF).T
    gqkv_ref[...] = (dot(x_ref[...], mixed, 0, 0) * FACTOR).astype(BF)
    window = (grad_middle + dot(mixed, qkv_ref[...], 1, 1)).astype(BF).reshape(WIN, WIN, D)
    own_ref[...] = window[:HALF, :HALF]
    right_ref[...] = window[:HALF, HALF:]
    down_ref[...] = window[HALF:, :HALF]
    diag_ref[...] = window[HALF:, HALF:]

    low = low_half((HEADS, LANES))
    even = jnp.zeros((HEADS, LANES), F4)
    odd = jnp.zeros((HEADS, LANES), F4)
    for c in range(WIN):
        part = wide_s[:, c, :]
        even += pltpu.roll(jnp.where(low, part, 0.0), (15 - c) % LANES, 1)
        odd += pltpu.roll(jnp.where(low, 0.0, part), (LANES - 1 - c) % LANES, 1)
    coords, valid = offset_coords()
    squashed = squashed_ref[...]
    table = jnp.concatenate([even, odd], 1) * 16.0 * squashed * (1.0 - squashed) * FACTOR
    table = jnp.where(valid[:1], table, 0.0)
    before = before_ref[...]
    gexit_ref[...] = dot(jnp.maximum(before, 0.0), table, 1, 1, TOP)
    grad_pos = jnp.where(before > 0.0, dot(exit_ref[...], table, 1, 0, TOP), 0.0)
    gentry_ref[...] = dot(coords, grad_pos, 1, 1, TOP)


def shape(*dims, dtype=F4):
    return jax.ShapeDtypeStruct(dims, dtype)


def vmem(*dims, dtype=F4):
    return pltpu.VMEM(dims, dtype)


def whole(count, scalar=()):
    return [
        pl.BlockSpec(memory_space=pltpu.SMEM if i in scalar else pltpu.VMEM) for i in range(count)
    ]


def device_index(row, col):
    return (row % 16) * 16 + col % 16


def moved(block, rows, cols):
    route = [
        (device_index(r, c), device_index(r + rows, c + cols)) for r in range(16) for c in range(16)
    ]
    return lax.ppermute(block, ALL, route)


def reduced(term):
    return lax.psum_scatter(term, ALL, scatter_dimension=0, tiled=True)


def local(
    tokens, cotangent, regions, qkv_weight, query_bias, value_bias, logit_scale,
    entry_weight, entry_bias, exit_weight, proj_weight, proj_bias, attn_gain, attn_shift,
    hidden_weight, hidden_bias, output_weight, output_bias, mlp_gain,
):
    row = lambda v: v.reshape(1, -1)
    both = jnp.concatenate([tokens, cotangent], 0)
    down = moved(both[:, :HALF, HALF:], -1, 0)
    right = moved(both[:, HALF:, :HALF], 0, -1)
    diag = moved(both[:, :HALF, :HALF], -1, -1)
    wide, squashed, before = pl.pallas_call(
        bias_kernel,
        out_shape=(
            shape(HEADS, WIN, LANES), shape(HEADS, 2 * LANES), shape(D, 2 * LANES),
        ),
        in_specs=whole(3),
        out_specs=tuple(whole(3)),
        scratch_shapes=[vmem(WIN, HEADS, LANES)],
        compiler_params=PARAMS,
        name="bias",
    )(entry_weight, row(entry_bias), exit_weight)
    (
        x, probs, qunit, kunit, inverse, value, att, normed, ainverse, gmiddle,
        mlp_vectors, hidden_sum, grad_hidden, grad_output,
    ) = pl.pallas_call(
        forward_kernel,
        out_shape=(
            shape(T, D, dtype=BF), shape(HEADS, T, T), shape(D, T), shape(D, T),
            shape(2, HEADS, 1, T), shape(D, T, dtype=BF), shape(D, T, dtype=BF),
            shape(T, D), shape(T, 1), shape(T, D), shape(3, D), shape(1, FF),
            shape(D, FF, dtype=BF), shape(FF, D, dtype=BF),
        ),
        in_specs=whole(19, (9,)),
        out_specs=tuple(whole(14)),
        scratch_shapes=[
            vmem(D, T, dtype=BF), vmem(D, T, dtype=BF), vmem(T, FF, dtype=BF), vmem(T, FF),
        ],
        compiler_params=PARAMS,
        name="forward",
    )(
        both, down, right, diag, row(regions), wide,
        qkv_weight, row(query_bias), row(value_bias), logit_scale,
        proj_weight, row(proj_bias), row(attn_gain), row(attn_shift),
        hidden_weight, row(hidden_bias), output_weight, row(output_bias), row(mlp_gain),
    )
    sum_hidden = reduced(grad_hidden.reshape(-1))
    sum_output = reduced(grad_output.reshape(-1))
    (
        grad_qkv, grad_proj, back_own, back_down, back_right, back_diag,
        vectors, grad_logit, grad_entry, grad_exit,
    ) = pl.pallas_call(
        backward_kernel,
        out_shape=(
            shape(D, 3 * D, dtype=BF), shape(D, D, dtype=BF),
            shape(HALF, HALF, D, dtype=BF), shape(HALF, HALF, D, dtype=BF),
            shape(HALF, HALF, D, dtype=BF), shape(HALF, HALF, D, dtype=BF),
            shape(8, D), shape(HEADS, 128), shape(8, D), shape(D, HEADS),
        ),
        in_specs=whole(18, (11,)),
        out_specs=tuple(whole(10)),
        scratch_shapes=[
            vmem(D, T, dtype=BF), vmem(D, T, dtype=BF), vmem(D, T, dtype=BF),
            vmem(3 * D, T), vmem(HEADS, WIN, LANES),
        ],
        compiler_params=PARAMS,
        name="backward",
    )(
        x, probs, qunit, kunit, inverse, value, att, normed, ainverse, gmiddle,
        qkv_weight, logit_scale, proj_weight, row(attn_gain),
        entry_weight, exit_weight, squashed, before,
    )
    sum_qkv = reduced(grad_qkv.reshape(-1))
    sum_proj = reduced(grad_proj.reshape(-1))
    from_above = moved(back_down, 1, 0)
    from_left = moved(back_right, 0, 1)
    from_diag = moved(back_diag, 1, 1)
    grad_tokens = jnp.concatenate(
        [
            jnp.concatenate([from_diag, from_above], 1),
            jnp.concatenate([from_left, back_own], 1),
        ],
        0,
    )[None]
    total_vectors, mlp_total, total_hidden, total_logit, first, second = lax.psum(
        (vectors[:5], mlp_vectors, hidden_sum, grad_logit[:, 0], grad_entry[:3], grad_exit), ALL
    )
    return (
        grad_tokens,
        sum_qkv.astype(F4),
        sum_proj.astype(F4),
        sum_hidden.astype(F4),
        sum_output.astype(F4),
        jnp.concatenate([total_vectors, mlp_total], 0),
        total_hidden.reshape(-1),
        total_logit,
        first,
        second,
    )


def solution(mesh):
    fine = Mesh(mesh.devices.reshape([n for _, n in AXES]), ALL)
    tile = P(None, ("z", "yh"), ("yl", "x", "core"))
    return jax.shard_map(
        local,
        mesh=fine,
        in_specs=(tile, tile, tile) + (P(),) * 16,
        out_specs=(tile,) + (P(ALL),) * 4 + (P(),) * 5,
        check_vma=False,
    )
```

```python
import math

import jax
import jax.numpy as jnp
from jax import lax
from jax.experimental import pallas as pl
from jax.experimental.pallas import tpu as pltpu
from jax.sharding import Mesh
from jax.sharding import PartitionSpec as P

WIN = 16
HALF = 8
T = 256
D = 512
HEADS = 16
E = 32
FF = 2048
CH = 512
LANES = 512
ALL = ("z", "yh", "yl", "x", "core")
AXES = (("z", 8), ("yh", 2), ("yl", 2), ("x", 4), ("core", 2))
PLANE = 16
PLANE_AXES = ALL[1:4]
FACTOR = 1.0 / 256.0
LOG_CAP = math.log(100.0)
TOP = lax.Precision.HIGHEST
BF = jnp.bfloat16
F4 = jnp.float32
PARAMS = pltpu.CompilerParams(vmem_limit_bytes=56 * 1024 * 1024)


def dot(a, b, ca, cb, precision=None):
    return lax.dot_general(
        a, b, (((ca,), (cb,)), ((), ())), precision=precision, preferred_element_type=F4
    )


def layer_stats(inputs):
    center = inputs - jnp.mean(inputs, -1, keepdims=True)
    inverse = lax.rsqrt(jnp.mean(center * center, -1, keepdims=True) + 1e-05)
    return center * inverse, inverse


def layer_back(upstream, normed, inverse, gain):
    scaled = upstream * gain
    inner = (
        scaled
        - jnp.mean(scaled, -1, keepdims=True)
        - normed * jnp.mean(scaled * normed, -1, keepdims=True)
    )
    return inverse * inner


def col_sum(block):
    return jnp.sum(block, 0, keepdims=True)


def offset_coords():
    lane = lax.broadcasted_iota(jnp.int32, (8, 2 * LANES), 1)
    parity = lane // LANES
    rest = lane - parity * LANES
    pair = rest // 32
    first = 2 * pair + parity
    second = rest - pair * 32
    valid = (first < 31) & (second < 31)

    def logged(index):
        u = (index.astype(F4) - 15.0) / 15.0 * 8.0
        size = jnp.log2(jnp.abs(u) + 1.0) / 3.0
        return jnp.where(u > 0.0, size, jnp.where(u < 0.0, -size, 0.0))

    row = lax.broadcasted_iota(jnp.int32, (8, 2 * LANES), 0)
    coords = jnp.where(
        row == 0, logged(first), jnp.where(row == 1, logged(second), jnp.where(row == 2, 1.0, 0.0))
    )
    return coords, valid


def low_half(shape):
    lane = lax.broadcasted_iota(jnp.int32, shape, len(shape) - 1)
    return lane % 32 < 16


def stack_rows(entry, bias):
    return jnp.concatenate([entry, bias, jnp.zeros((5, entry.shape[1]), F4)], 0)


def spread(ref, block, part, term):
    for lane in range(0, term.shape[1], 128):
        ref[block + lane // 128, pl.ds(part, D, stride=4), :] = term[:, lane : lane + 128]


def joined(ref):
    return jnp.concatenate([ref[b] for b in range(4)], 1)


def ordered(term, core, lines=slice(None)):
    parts = term.reshape(8, PLANE, 2, 8, term.shape[1])
    if lines != slice(None):
        parts = parts.reshape(4, 2, PLANE, 2, 8, term.shape[1])[:, lines]
    cut = [parts[:, i, core] for i in range(PLANE)]
    return jnp.concatenate(cut, 0).reshape(-1, term.shape[1])


def split_cores(core, first, second, keep_ref, send_ref, start):
    rows = pl.ds(start, first.shape[0])
    keep_ref[rows, :] = jnp.where(core == 0, first, second).astype(BF)
    send_ref[rows, :] = jnp.where(core == 0, second, first).astype(BF)


def two_parts(value):
    high = value.astype(BF)
    low = (value - high.astype(F4)).astype(BF)
    return high, low


def wide_parts(value):
    high, low = two_parts(value)
    return jnp.concatenate([high.astype(F4), low.astype(F4), jnp.zeros((8, 256), F4)], 1)


def gather_kernel(keep_ref, got_ref, okeep_ref, ogot_ref, small_ref, sgot_ref, out_ref):
    for i in range(PLANE):
        rows = slice(64 * i, 64 * i + 64)
        out_ref[i, :64] = (keep_ref[rows].astype(F4) + got_ref[rows].astype(F4)).astype(BF)
        rows = slice(32 * i, 32 * i + 32)
        out_ref[i, 64:96] = (okeep_ref[rows].astype(F4) + ogot_ref[rows].astype(F4)).astype(BF)
        small = small_ref[8 * i : 8 * i + 8] + sgot_ref[8 * i : 8 * i + 8]
        part = jnp.concatenate([wide_parts(small), jnp.zeros((8, D), F4)], 0)
        out_ref[i, 96:] = part.astype(BF)


def line_kernel(early_ref, late_ref, line_ref, out_ref):
    hidden = jnp.sum(early_ref[...].astype(F4), 0).reshape(8, 8, D)
    late = jnp.sum(late_ref[...].astype(F4), 0)
    mixed = late[:64].reshape(8, 8, D)
    output = late[64:96].reshape(4, 8, D)
    small = wide_parts(late[96:104, :128] + late[96:104, 128:256])
    for z in range(8):
        mine = jnp.where(line_ref[0] % 2 == z % 2, output[z // 2], 0.0)
        out_ref[z] = jnp.concatenate([hidden[z], mine, mixed[z], small], 0).astype(BF)


def finish_kernel(blocks_ref, hidden_ref, output_ref, qkv_ref, proj_ref, small_ref):
    total = jnp.sum(blocks_ref[...].astype(F4), 0)
    hidden_ref[...] = total[:8]
    output_ref[...] = total[8:16]
    qkv_ref[...] = total[16:24, :384]
    proj_ref[...] = total[16:24, 384:]
    small = total[24:, :128] + total[24:, 128:256]
    small_ref[...] = jnp.broadcast_to(small[None], small_ref.shape)


def unpack_kernel(small_ref, vectors_ref, hidden_ref, logit_ref, first_ref, second_ref):
    rows = [small_ref[pl.ds(c, 32, stride=4), :] for c in range(4)]
    total = jnp.concatenate(rows, 1)
    vectors_ref[...] = total[:8]
    hidden_ref[...] = total[8:12]
    first_ref[...] = total[12:15]
    second_ref[...] = total[15:31]
    logit_ref[...] = total[31:, :128]


def bias_kernel(entry_ref, mid_ref, exit_ref, wide_ref, squashed_ref, before_ref, scratch):
    coords, _ = offset_coords()
    before = dot(stack_rows(entry_ref[...], mid_ref[...]), coords, 0, 0, TOP)
    before_ref[...] = before
    hidden = jnp.maximum(before, 0.0)
    squashed = jax.nn.sigmoid(dot(exit_ref[...], hidden, 1, 0, TOP))
    squashed_ref[...] = squashed
    table = 16.0 * squashed
    even, odd = table[:, :LANES], table[:, LANES:]
    low = low_half((HEADS, LANES))
    for c in range(WIN):
        scratch[c] = jnp.where(
            low,
            pltpu.roll(even, (c - 15) % LANES, 1),
            pltpu.roll(odd, (c + 1) % LANES, 1),
        )
    for h in range(HEADS):
        wide_ref[h] = scratch[:, h, :]


def forward_kernel(
    tokens_ref, cotangent_ref, down_ref, right_ref, diag_ref, regions_ref, wide_ref,
    qkv_ref, qbias_ref, vbias_ref, logit_ref,
    proj_ref, pbias_ref, again_ref, ashift_ref,
    hidden_ref, hbias_ref, output_ref, obias_ref, mgain_ref, core_ref, line_ref,
    x_ref, probs_ref, qunit_ref, kunit_ref, inverse_ref, value_ref, att_ref,
    normed_ref, ainverse_ref, gmiddle_ref, vectors_ref, hsum_ref, keep_ref, send_ref,
    qlow_s, klow_s, act_s, slope_s, ghidden_s, goutput_s,
):
    def assemble(own_ref, i):
        top = jnp.concatenate([own_ref[0, HALF:, HALF:], right_ref[i]], 1)
        bottom = jnp.concatenate([down_ref[i], diag_ref[i]], 1)
        return jnp.concatenate([top, bottom], 0).reshape(T, D)

    x = assemble(tokens_ref, 0)
    x_ref[...] = x
    mixed = dot(x, qkv_ref[...], 1, 0)
    q = (mixed[:, :D] + qbias_ref[...]).T
    k = mixed[:, D : 2 * D].T
    value_ref[...] = (mixed[:, 2 * D :] + vbias_ref[...]).T.astype(BF)
    for index, (raw, unit_ref, low_s) in enumerate(
        ((q, qunit_ref, qlow_s), (k, kunit_ref, klow_s))
    ):
        split = raw.reshape(HEADS, E, T)
        inverse = lax.rsqrt(jnp.sum(split * split, 1, keepdims=True) + 1e-06)
        inverse_ref[index] = inverse
        unit = (split * inverse).reshape(D, T)
        unit_ref[...] = unit
        low_s[...] = unit.astype(BF)
    region_row = regions_ref[...]
    region_col = jnp.broadcast_to(region_row.astype(F4), (8, T)).T[:, :1]
    allowed = region_col == region_row.astype(F4)

    def head(h, carry):
        at = pl.ds(pl.multiple_of(h * E, E), E)
        scale = jnp.exp(jnp.minimum(jnp.full((1, T), logit_ref[h], F4), LOG_CAP))
        cosine = dot(klow_s[at, :], qlow_s[at, :], 0, 0)
        wide = wide_ref[h]
        rolled = [wide] + [pltpu.roll(wide, LANES - 16 * p, 1) for p in range(1, 8)]
        bias = jnp.concatenate(
            [
                rolled[(15 - r) % 8][:, (15 - r) // 8 * 128 : (15 - r) // 8 * 128 + T]
                for r in range(WIN)
            ],
            0,
        )
        logits = jnp.where(allowed, scale * cosine + bias, -1000000000.0)
        powers = jnp.exp(logits - jnp.max(logits, 0, keepdims=True))
        probs = powers / jnp.sum(powers, 0, keepdims=True)
        probs_ref[h] = probs
        att_ref[at, :] = dot(value_ref[at, :], probs.astype(BF), 1, 0).astype(BF)
        return carry

    lax.fori_loop(0, HEADS, head, 0, unroll=2)

    projected = dot(att_ref[...], proj_ref[...], 0, 0) + pbias_ref[...]
    attn_normed, attn_inverse = layer_stats(projected)
    normed_ref[...] = attn_normed
    ainverse_ref[...] = attn_inverse
    middle = x.astype(F4) + (attn_normed * again_ref[...] + ashift_ref[...])
    middle_low = middle.astype(BF)
    emitted = jnp.zeros((T, D), F4)
    for c in range(0, FF, CH):
        cut = slice(c, c + CH)
        before = dot(middle_low, hidden_ref[:, cut], 1, 0) + hbias_ref[:, cut]
        cumulative = 0.5 * (1.0 + lax.erf(before * (1.0 / math.sqrt(2.0))))
        density = jnp.exp(-0.5 * before * before) * (1.0 / math.sqrt(2.0 * math.pi))
        slope_s[:, cut] = cumulative + before * density
        act = (before * cumulative).astype(BF)
        act_s[:, cut] = act
        emitted += dot(act, output_ref[cut, :], 1, 0)
    normed, inverse = layer_stats(emitted + obias_ref[...])
    incoming = assemble(cotangent_ref, 1).astype(F4)
    grad_emitted = layer_back(incoming, normed, inverse, mgain_ref[...])
    emitted_low = grad_emitted.astype(BF)
    vectors_ref[0:1, :] = col_sum(grad_emitted) * FACTOR
    vectors_ref[1:2, :] = col_sum(incoming * normed) * FACTOR
    vectors_ref[2:3, :] = col_sum(incoming) * FACTOR
    grad_middle = incoming
    for c in range(0, FF, CH):
        cut = slice(c, c + CH)
        grad_act = dot(emitted_low, output_ref[cut, :], 1, 1)
        grad_before = grad_act * slope_s[:, cut]
        hsum_ref[:, cut] = col_sum(grad_before) * FACTOR
        before_low = grad_before.astype(BF)
        goutput_s[cut, :] = dot(act_s[:, cut], emitted_low, 0, 0) * FACTOR
        spread(ghidden_s, 0, c // CH, dot(middle_low, before_low, 0, 0) * FACTOR)
        grad_middle += dot(before_low, hidden_ref[:, cut], 1, 1)
    gmiddle_ref[...] = grad_middle
    core = core_ref[0]
    term = joined(ghidden_s)
    split_cores(core, ordered(term, 0), ordered(term, 1), keep_ref, send_ref, 0)
    term = goutput_s[...]
    even = line_ref[0] % 2 == 0
    halves = [[ordered(term, k, lines) for lines in range(2)] for k in range(2)]
    near = [jnp.where(even, a, b) for a, b in halves]
    far = [jnp.where(even, b, a) for a, b in halves]
    split_cores(core, *near, keep_ref, send_ref, FF // 2)
    split_cores(core, *far, keep_ref, send_ref, FF // 4 * 3)


def middle_kernel(
    att_ref, normed_ref, ainverse_ref, gmiddle_ref, proj_ref, again_ref,
    gatt_ref, gproj_ref, vectors_ref,
):
    grad_middle = gmiddle_ref[...]
    attn_normed = normed_ref[...]
    grad_projected = layer_back(grad_middle, attn_normed, ainverse_ref[...], again_ref[...])
    projected_low = grad_projected.astype(BF)
    gatt_ref[...] = dot(proj_ref[...], projected_low, 1, 1).astype(BF)
    vectors_ref[0:1, :] = col_sum(grad_projected) * FACTOR
    vectors_ref[1:2, :] = col_sum(grad_middle * attn_normed) * FACTOR
    vectors_ref[2:3, :] = col_sum(grad_middle) * FACTOR
    grad_proj = dot(att_ref[...], projected_low, 1, 0) * FACTOR
    for c in range(4):
        gproj_ref[pl.ds(c, D, stride=4), :] = grad_proj[:, c * 128 : (c + 1) * 128]


def backward_kernel(
    x_ref, probs_ref, qunit_ref, kunit_ref, inverse_ref, value_ref, gatt_s, gproj_ref,
    gmiddle_ref, qkv_ref, logit_ref, entry_ref, exit_ref, squashed_ref, before_ref,
    attn_ref, mlp_ref, hsum_ref, core_ref,
    keep_ref, send_ref, own_ref, down_ref, right_ref, diag_ref, small_ref,
    qlow_s, klow_s, gmixed_s, wide_s, grads_s, small_s,
):
    small_s[2:5, :] = attn_ref[...]
    small_s[5:8, :] = mlp_ref[...]
    for c in range(0, FF, D):
        small_s[8 + c // D : 9 + c // D, :] = hsum_ref[:, c : c + D]
    qlow_s[...] = qunit_ref[...].astype(BF)
    klow_s[...] = kunit_ref[...].astype(BF)

    def head(h, carry):
        at = pl.ds(pl.multiple_of(h * E, E), E)
        kat = pl.ds(pl.multiple_of(h * E + D, E), E)
        vat = pl.ds(pl.multiple_of(h * E + 2 * D, E), E)
        scale = jnp.exp(jnp.minimum(jnp.full((1, T), logit_ref[h], F4), LOG_CAP))
        qlow, klow, gatt = qlow_s[at, :], klow_s[at, :], gatt_s[at, :]
        probs = probs_ref[h]
        grad_probs = dot(value_ref[at, :], gatt, 0, 0)
        gmixed_s[vat, :] = dot(gatt, probs.astype(BF), 1, 1)
        grad_scores = probs * (grad_probs - jnp.sum(probs * grad_probs, 0, keepdims=True))
        cosine = dot(klow, qlow, 0, 0)
        live = jnp.full((1, T), logit_ref[h], F4) < LOG_CAP
        total = jnp.sum(jnp.sum(grad_scores * cosine, 0, keepdims=True), 1, keepdims=True)
        term = jnp.where(live, total * scale * FACTOR, 0.0)
        lane = lax.broadcasted_iota(jnp.int32, (1, T), 1)
        carry = carry + jnp.where(lane == h, term, 0.0)
        grad_cosine = (grad_scores * scale).astype(BF)
        for index, (part, unit_ref, where) in enumerate(
            (
                (dot(klow, grad_cosine, 1, 0), qunit_ref, at),
                (dot(qlow, grad_cosine, 1, 1), kunit_ref, kat),
            )
        ):
            unit = unit_ref[at, :]
            gmixed_s[where, :] = inverse_ref[index, h] * (
                part - unit * jnp.sum(unit * part, 0, keepdims=True)
            )
        wide = None
        for p in range(8):
            first = grad_scores[(15 - p) * 16 : (16 - p) * 16]
            second = grad_scores[(7 - p) * 16 : (8 - p) * 16]
            blank = jnp.zeros((WIN, 128), F4)
            placed = jnp.concatenate(
                [first[:, :128], first[:, 128:] + second[:, :128], second[:, 128:], blank], 1
            )
            if p:
                placed = pltpu.roll(placed, 16 * p, 1)
            wide = placed if wide is None else wide + placed
        wide_s[h] = wide
        return carry

    logits = lax.fori_loop(0, HEADS, head, jnp.zeros((1, T), F4), unroll=2)
    small_s[31:32, :] = jnp.concatenate([logits, jnp.zeros((1, D - T), F4)], 1)

    ones = jnp.ones((8, T), F4)
    small_s[0:1, :] = dot(ones, gmixed_s[0:D, :], 1, 1, TOP)[:1] * FACTOR
    small_s[1:2, :] = dot(ones, gmixed_s[2 * D :, :], 1, 1, TOP)[:1] * FACTOR
    mixed = gmixed_s[...].astype(BF).T
    for c in range(4):
        cut = slice(c * 384, (c + 1) * 384)
        spread(grads_s, 0, c, dot(x_ref[...], mixed[:, cut], 0, 0) * FACTOR)
    grads = jnp.concatenate([grads_s[0], grads_s[1], grads_s[2], gproj_ref[...]], 1)
    split_cores(core_ref[0], ordered(grads, 0), ordered(grads, 1), keep_ref, send_ref, 0)
    window = (gmiddle_ref[...] + dot(mixed, qkv_ref[...], 1, 1)).astype(BF).reshape(WIN, WIN, D)
    own_ref[...] = window[:HALF, :HALF]
    right_ref[...] = window[:HALF, HALF:]
    down_ref[...] = window[HALF:, :HALF]
    diag_ref[...] = window[HALF:, HALF:]

    low = low_half((HEADS, LANES))
    even = jnp.zeros((HEADS, LANES), F4)
    odd = jnp.zeros((HEADS, LANES), F4)
    for c in range(WIN):
        part = wide_s[:, c, :]
        even += pltpu.roll(jnp.where(low, part, 0.0), (15 - c) % LANES, 1)
        odd += pltpu.roll(jnp.where(low, 0.0, part), (LANES - 1 - c) % LANES, 1)
    coords, valid = offset_coords()
    squashed = squashed_ref[...]
    table = jnp.concatenate([even, odd], 1) * 16.0 * squashed * (1.0 - squashed) * FACTOR
    table = jnp.where(valid[:1], table, 0.0)
    before = before_ref[...]
    small_s[15:31, :] = dot(table, jnp.maximum(before, 0.0), 1, 1, TOP)
    grad_pos = jnp.where(before > 0.0, dot(exit_ref[...], table, 0, 0, TOP), 0.0)
    small_s[12:15, :] = dot(coords, grad_pos, 1, 1, TOP)[:3]
    small = small_s[...]
    for c in range(4):
        small_ref[pl.ds(c, 32, stride=4), :] = small[:, c * 128 : (c + 1) * 128]


def shape(*dims, dtype=F4):
    return jax.ShapeDtypeStruct(dims, dtype)


def vmem(*dims, dtype=F4):
    return pltpu.VMEM(dims, dtype)


def whole(count, scalar=()):
    return [
        pl.BlockSpec(memory_space=pltpu.SMEM if i in scalar else pltpu.VMEM) for i in range(count)
    ]


def device_index(row, col):
    return (row % 16) * 16 + col % 16


def moved(block, rows, cols):
    route = [
        (device_index(r, c), device_index(r + rows, c + cols)) for r in range(16) for c in range(16)
    ]
    return lax.ppermute(block, ALL, route)


def swapped(block):
    return lax.ppermute(block, "core", [(0, 1), (1, 0)])


def joint(keep, got):
    return (keep.astype(F4) + got.astype(F4)).astype(BF)


def exchanged(blocks, axes):
    return lax.all_to_all(blocks, axes, 0, 0)


def across(block):
    return lax.ppermute(block, "z", [(i, i ^ 1) for i in range(8)])


def cost(us):
    return pl.CostEstimate(flops=int(us * 5e8), bytes_accessed=int(us * 2e6), transcendentals=0)


def local(
    tokens, cotangent, regions, qkv_weight, query_bias, value_bias, logit_scale,
    entry_weight, entry_bias, exit_weight, proj_weight, proj_bias, attn_gain, attn_shift,
    hidden_weight, hidden_bias, output_weight, output_bias, mlp_gain,
):
    row = lambda v: v.reshape(1, -1)

    def strip(rows, cols):
        return jnp.concatenate([tokens[:, rows, cols], cotangent[:, rows, cols]], 0)

    head, tail = slice(0, HALF), slice(HALF, WIN)
    down = moved(strip(head, tail), -1, 0)
    right = moved(strip(tail, head), 0, -1)
    diag = moved(strip(head, head), -1, -1)
    exit_turned = exit_weight.T
    wide, squashed, before = pl.pallas_call(
        bias_kernel,
        out_shape=(
            shape(HEADS, WIN, LANES), shape(HEADS, 2 * LANES), shape(D, 2 * LANES),
        ),
        in_specs=whole(3),
        out_specs=tuple(whole(3)),
        scratch_shapes=[vmem(WIN, HEADS, LANES)],
        compiler_params=PARAMS,
        cost_estimate=cost(5),
        name="bias",
    )(entry_weight, row(entry_bias), exit_turned)
    core = lax.axis_index("core").astype(jnp.int32).reshape(1)
    line = lax.axis_index("z").astype(jnp.int32).reshape(1)
    (
        x, probs, qunit, kunit, inverse, value, att, normed, ainverse, gmiddle,
        mlp_vectors, hidden_sum, keep, send,
    ) = pl.pallas_call(
        forward_kernel,
        out_shape=(
            shape(T, D, dtype=BF), shape(HEADS, T, T), shape(D, T), shape(D, T),
            shape(2, HEADS, 1, T), shape(D, T, dtype=BF), shape(D, T, dtype=BF),
            shape(T, D), shape(T, 1), shape(T, D), shape(3, D), shape(1, FF),
            shape(FF, D, dtype=BF), shape(FF, D, dtype=BF),
        ),
        in_specs=whole(22, (10, 20, 21)),
        out_specs=tuple(whole(14)),
        scratch_shapes=[
            vmem(D, T, dtype=BF), vmem(D, T, dtype=BF), vmem(T, FF, dtype=BF), vmem(T, FF),
            vmem(4, FF, 128), vmem(FF, D),
        ],
        compiler_params=PARAMS,
        cost_estimate=cost(17),
        name="forward",
    )(
        tokens, cotangent, down, right, diag, row(regions), wide,
        qkv_weight, row(query_bias), row(value_bias), logit_scale,
        proj_weight, row(proj_bias), row(attn_gain), row(attn_shift),
        hidden_weight, row(hidden_bias), output_weight, row(output_bias), row(mlp_gain), core, line,
    )
    got = swapped(send)
    grad_att, grad_proj, attn_vectors = pl.pallas_call(
        middle_kernel,
        out_shape=(shape(D, T, dtype=BF), shape(FF, 128), shape(3, D)),
        in_specs=whole(6),
        out_specs=tuple(whole(3)),
        compiler_params=PARAMS,
        cost_estimate=cost(4),
        name="middle",
    )(att, normed, ainverse, gmiddle, proj_weight, row(attn_gain))
    early = joint(keep[: FF // 2], got[: FF // 2])
    far = joint(keep[FF // 4 * 3 :], got[FF // 4 * 3 :])
    near = joint(keep[FF // 2 : FF // 4 * 3], got[FF // 2 : FF // 4 * 3])
    early, far, near, grad_att = lax.optimization_barrier((early, far, near, grad_att))
    far = across(far)
    early = exchanged(early.reshape(PLANE, -1, D), PLANE_AXES)
    keep, send, back_own, back_down, back_right, back_diag, small = pl.pallas_call(
        backward_kernel,
        out_shape=(
            shape(FF // 2, D, dtype=BF), shape(FF // 2, D, dtype=BF),
            shape(HALF, HALF, D, dtype=BF), shape(HALF, HALF, D, dtype=BF),
            shape(HALF, HALF, D, dtype=BF), shape(HALF, HALF, D, dtype=BF),
            shape(128, 128),
        ),
        in_specs=whole(19, (10, 18)),
        out_specs=tuple(whole(7)),
        scratch_shapes=[
            vmem(D, T, dtype=BF), vmem(D, T, dtype=BF), vmem(3 * D, T),
            vmem(HEADS, WIN, LANES), vmem(3, FF, 128), vmem(32, D),
        ],
        compiler_params=PARAMS,
        cost_estimate=cost(17),
        name="backward",
    )(
        x, probs, qunit, kunit, inverse, value, grad_att, grad_proj, gmiddle,
        qkv_weight, logit_scale, entry_weight, exit_turned, squashed, before,
        attn_vectors, mlp_vectors, hidden_sum, core,
    )
    late = pl.pallas_call(
        gather_kernel,
        out_shape=shape(PLANE, 112, D, dtype=BF),
        in_specs=whole(6),
        out_specs=whole(1)[0],
        compiler_params=PARAMS,
        cost_estimate=cost(2),
        name="gather",
    )(keep, swapped(send), near, far, small, swapped(small))
    late = exchanged(late, PLANE_AXES)
    from_above = moved(back_down, 1, 0)
    from_left = moved(back_right, 0, 1)
    from_diag = moved(back_diag, 1, 1)
    blocks = pl.pallas_call(
        line_kernel,
        out_shape=shape(8, 32, D, dtype=BF),
        in_specs=whole(3, (2,)),
        out_specs=whole(1)[0],
        compiler_params=PARAMS,
        cost_estimate=cost(2),
        name="line",
    )(early, late, line)
    sum_hidden, sum_output, sum_qkv, sum_proj, small = pl.pallas_call(
        finish_kernel,
        out_shape=(shape(8, D), shape(8, D), shape(8, 384), shape(8, 128), shape(PLANE, 8, 128)),
        in_specs=whole(1),
        out_specs=tuple(whole(5)),
        compiler_params=PARAMS,
        cost_estimate=cost(1),
        name="finish",
    )(exchanged(blocks, "z"))
    small = exchanged(small, PLANE_AXES).reshape(128, 128)
    vectors, hidden_total, logit_total, first, second = pl.pallas_call(
        unpack_kernel,
        out_shape=(shape(8, D), shape(4, D), shape(1, 128), shape(3, D), shape(HEADS, D)),
        in_specs=whole(1),
        out_specs=tuple(whole(5)),
        compiler_params=PARAMS,
        cost_estimate=cost(1),
        name="unpack",
    )(small)
    grad_tokens = jnp.concatenate(
        [
            jnp.concatenate([from_diag, from_above], 1),
            jnp.concatenate([from_left, back_own], 1),
        ],
        0,
    )[None]
    return (
        grad_tokens,
        sum_qkv.reshape(-1),
        sum_proj.reshape(-1),
        sum_hidden.reshape(-1),
        sum_output.reshape(-1),
        vectors,
        hidden_total.reshape(-1),
        logit_total[0, :HEADS],
        first,
        second.T,
    )


def solution(mesh):
    fine = Mesh(mesh.devices.reshape([n for _, n in AXES]), ALL)
    tile = P(None, ("z", "yh"), ("yl", "x", "core"))
    return jax.shard_map(
        local,
        mesh=fine,
        in_specs=(tile, tile, tile) + (P(),) * 16,
        out_specs=(tile,) + (P(ALL),) * 4 + (P(),) * 5,
        check_vma=False,
    )
```

```python
import math

import jax
import jax.numpy as jnp
from jax import lax
from jax.experimental import pallas as pl
from jax.experimental.pallas import tpu as pltpu
from jax.sharding import Mesh
from jax.sharding import PartitionSpec as P

WIN = 16
HALF = 8
T = 256
D = 512
HEADS = 16
E = 32
FF = 2048
CH = 512
LANES = 512
ALL = ("z", "yh", "yl", "x", "core")
AXES = (("z", 8), ("yh", 2), ("yl", 2), ("x", 4), ("core", 2))
PLANE = 16
PLANE_AXES = ALL[1:4]
FACTOR = 1.0 / 256.0
LOG_CAP = math.log(100.0)
TOP = lax.Precision.HIGHEST
BF = jnp.bfloat16
F4 = jnp.float32
PARAMS = pltpu.CompilerParams(vmem_limit_bytes=56 * 1024 * 1024)


def dot(a, b, ca, cb, precision=None):
    return lax.dot_general(
        a, b, (((ca,), (cb,)), ((), ())), precision=precision, preferred_element_type=F4
    )


def layer_stats(inputs):
    center = inputs - jnp.mean(inputs, -1, keepdims=True)
    inverse = lax.rsqrt(jnp.mean(center * center, -1, keepdims=True) + 1e-05)
    return center * inverse, inverse


def layer_back(upstream, normed, inverse, gain):
    scaled = upstream * gain
    inner = (
        scaled
        - jnp.mean(scaled, -1, keepdims=True)
        - normed * jnp.mean(scaled * normed, -1, keepdims=True)
    )
    return inverse * inner


def col_sum(block):
    return jnp.sum(block, 0, keepdims=True)


def offset_coords():
    lane = lax.broadcasted_iota(jnp.int32, (8, 2 * LANES), 1)
    parity = lane // LANES
    rest = lane - parity * LANES
    pair = rest // 32
    first = 2 * pair + parity
    second = rest - pair * 32
    valid = (first < 31) & (second < 31)

    def logged(index):
        u = (index.astype(F4) - 15.0) / 15.0 * 8.0
        size = jnp.log2(jnp.abs(u) + 1.0) / 3.0
        return jnp.where(u > 0.0, size, jnp.where(u < 0.0, -size, 0.0))

    row = lax.broadcasted_iota(jnp.int32, (8, 2 * LANES), 0)
    coords = jnp.where(
        row == 0, logged(first), jnp.where(row == 1, logged(second), jnp.where(row == 2, 1.0, 0.0))
    )
    return coords, valid


def low_half(shape):
    lane = lax.broadcasted_iota(jnp.int32, shape, len(shape) - 1)
    return lane % 32 < 16


def stack_rows(entry, bias):
    return jnp.concatenate([entry, bias, jnp.zeros((5, entry.shape[1]), F4)], 0)


def spread(ref, block, part, term):
    for lane in range(0, term.shape[1], 128):
        ref[block + lane // 128, pl.ds(part, D, stride=4), :] = term[:, lane : lane + 128]


def joined(ref):
    return jnp.concatenate([ref[b] for b in range(4)], 1)


def ordered(term, core, lines=slice(None)):
    parts = term.reshape(8, PLANE, 2, 8, term.shape[1])
    if lines != slice(None):
        parts = parts.reshape(4, 2, PLANE, 2, 8, term.shape[1])[:, lines]
    cut = [parts[:, i, core] for i in range(PLANE)]
    return jnp.concatenate(cut, 0).reshape(-1, term.shape[1])


def split_cores(core, first, second, keep_ref, send_ref, start):
    rows = pl.ds(start, first.shape[0])
    keep_ref[rows, :] = jnp.where(core == 0, first, second).astype(BF)
    send_ref[rows, :] = jnp.where(core == 0, second, first).astype(BF)


def line_kernel(early_ref, late_ref, line_ref, out_ref):
    hidden = early_ref[...].reshape(8, 8, D)
    late = jnp.sum(late_ref[...].astype(F4), 0)
    mixed = late[:64].reshape(8, 8, D)
    output = late[64:96].reshape(4, 8, D)
    for z in range(8):
        mine = jnp.where(line_ref[0] % 2 == z % 2, output[z // 2], 0.0)
        out_ref[z] = jnp.concatenate([hidden[z], mine, mixed[z]], 0).astype(BF)


def finish_kernel(blocks_ref, hidden_ref, output_ref, qkv_ref, proj_ref):
    total = jnp.sum(blocks_ref[...].astype(F4), 0)
    for r in range(8):
        hidden_ref[r * D : (r + 1) * D] = total[r]
        output_ref[r * D : (r + 1) * D] = total[8 + r]
        qkv_ref[r * 384 : (r + 1) * 384] = total[16 + r, :384]
        proj_ref[r * 128 : (r + 1) * 128] = total[16 + r, 384:]


def unpack_kernel(small_ref, vectors_ref, hidden_ref, logit_ref, first_ref, second_ref):
    rows = [small_ref[pl.ds(c, 32, stride=4), :] for c in range(4)]
    total = jnp.concatenate(rows, 1)
    vectors_ref[...] = total[:8]
    for c in range(4):
        hidden_ref[c * D : (c + 1) * D] = total[8 + c]
    first_ref[...] = total[12:15]
    second_ref[...] = total[15:31]
    logit_ref[...] = total[31, :HEADS]


def bias_kernel(entry_ref, mid_ref, exit_ref, wide_ref, squashed_ref, before_ref, scratch):
    coords, _ = offset_coords()
    before = dot(stack_rows(entry_ref[...], mid_ref[...]), coords, 0, 0, TOP)
    before_ref[...] = before
    hidden = jnp.maximum(before, 0.0)
    squashed = jax.nn.sigmoid(dot(exit_ref[...], hidden, 1, 0, TOP))
    squashed_ref[...] = squashed
    table = 16.0 * squashed
    even, odd = table[:, :LANES], table[:, LANES:]
    low = low_half((HEADS, LANES))
    for c in range(WIN):
        scratch[c] = jnp.where(
            low,
            pltpu.roll(even, (c - 15) % LANES, 1),
            pltpu.roll(odd, (c + 1) % LANES, 1),
        )
    for h in range(HEADS):
        wide_ref[h] = scratch[:, h, :]


def forward_kernel(
    tokens_ref, cotangent_ref, down_ref, right_ref, diag_ref, regions_ref, wide_ref,
    qkv_ref, qbias_ref, vbias_ref, logit_ref,
    proj_ref, pbias_ref, again_ref, ashift_ref,
    hidden_ref, hbias_ref, output_ref, obias_ref, mgain_ref, core_ref, line_ref,
    x_ref, probs_ref, qunit_ref, kunit_ref, inverse_ref, value_ref, att_ref,
    normed_ref, ainverse_ref, gmiddle_ref, vectors_ref, hsum_ref, keep_ref, send_ref,
    qlow_s, klow_s, act_s, slope_s, ghidden_s, goutput_s,
):
    def assemble(own_ref, i):
        top = jnp.concatenate([own_ref[0, HALF:, HALF:], right_ref[i]], 1)
        bottom = jnp.concatenate([down_ref[i], diag_ref[i]], 1)
        return jnp.concatenate([top, bottom], 0).reshape(T, D)

    x = assemble(tokens_ref, 0)
    x_ref[...] = x.T
    mixed = dot(x, qkv_ref[...], 1, 0)
    q = (mixed[:, :D] + qbias_ref[...]).T
    k = mixed[:, D : 2 * D].T
    value_ref[...] = (mixed[:, 2 * D :] + vbias_ref[...]).T.astype(BF)
    for index, (raw, unit_ref, low_s) in enumerate(
        ((q, qunit_ref, qlow_s), (k, kunit_ref, klow_s))
    ):
        split = raw.reshape(HEADS, E, T)
        inverse = lax.rsqrt(jnp.sum(split * split, 1, keepdims=True) + 1e-06)
        inverse_ref[index] = inverse
        unit = (split * inverse).reshape(D, T)
        unit_ref[...] = unit
        low_s[...] = unit.astype(BF)
    own_row = lax.broadcasted_iota(jnp.int32, (WIN, T), 0)
    token = lax.broadcasted_iota(jnp.int32, (WIN, T), 1)
    pick = jnp.where(token % WIN == own_row, 1.0, 0.0).astype(BF)
    by_row = dot(regions_ref[0].astype(F4).astype(BF), pick, 1, 0)
    region_row = col_sum(jnp.where(token // WIN == own_row, by_row, 0.0))
    region_col = jnp.broadcast_to(region_row, (8, T)).T[:, :1]
    allowed = region_col == region_row

    def head(h, carry):
        at = pl.ds(pl.multiple_of(h * E, E), E)
        scale = jnp.exp(jnp.minimum(jnp.full((1, T), logit_ref[h], F4), LOG_CAP))
        cosine = dot(klow_s[at, :], qlow_s[at, :], 0, 0)
        wide = wide_ref[h]
        rolled = [wide] + [pltpu.roll(wide, LANES - 16 * p, 1) for p in range(1, 8)]
        bias = jnp.concatenate(
            [
                rolled[(15 - r) % 8][:, (15 - r) // 8 * 128 : (15 - r) // 8 * 128 + T]
                for r in range(WIN)
            ],
            0,
        )
        logits = jnp.where(allowed, scale * cosine + bias, -1000000000.0)
        powers = jnp.exp(logits - jnp.max(logits, 0, keepdims=True))
        probs = powers / jnp.sum(powers, 0, keepdims=True)
        probs_ref[h] = probs
        att_ref[at, :] = dot(value_ref[at, :], probs.astype(BF), 1, 0).astype(BF)
        return carry

    lax.fori_loop(0, HEADS, head, 0, unroll=2)

    projected = dot(att_ref[...], proj_ref[...], 0, 0) + pbias_ref[...]
    attn_normed, attn_inverse = layer_stats(projected)
    normed_ref[...] = attn_normed
    ainverse_ref[...] = attn_inverse
    middle = x.astype(F4) + (attn_normed * again_ref[...] + ashift_ref[...])
    middle_low = middle.astype(BF)
    emitted = jnp.zeros((T, D), F4)
    for c in range(0, FF, CH):
        cut = slice(c, c + CH)
        before = dot(middle_low, hidden_ref[:, cut], 1, 0) + hbias_ref[:, cut]
        cumulative = 0.5 * (1.0 + lax.erf(before * (1.0 / math.sqrt(2.0))))
        density = jnp.exp(-0.5 * before * before) * (1.0 / math.sqrt(2.0 * math.pi))
        slope_s[:, cut] = cumulative + before * density
        act = (before * cumulative).astype(BF)
        act_s[:, cut] = act
        emitted += dot(act, output_ref[cut, :], 1, 0)
    normed, inverse = layer_stats(emitted + obias_ref[...])
    incoming = assemble(cotangent_ref, 1).astype(F4)
    grad_emitted = layer_back(incoming, normed, inverse, mgain_ref[...])
    emitted_low = grad_emitted.astype(BF)
    vectors_ref[0:1, :] = col_sum(grad_emitted) * FACTOR
    vectors_ref[1:2, :] = col_sum(incoming * normed) * FACTOR
    vectors_ref[2:3, :] = col_sum(incoming) * FACTOR
    grad_middle = incoming
    for c in range(0, FF, CH):
        cut = slice(c, c + CH)
        grad_act = dot(emitted_low, output_ref[cut, :], 1, 1)
        grad_before = grad_act * slope_s[:, cut]
        hsum_ref[:, cut] = col_sum(grad_before) * FACTOR
        before_low = grad_before.astype(BF)
        goutput_s[cut, :] = dot(act_s[:, cut], emitted_low, 0, 0) * FACTOR
        spread(ghidden_s, 0, c // CH, dot(middle_low, before_low, 0, 0) * FACTOR)
        grad_middle += dot(before_low, hidden_ref[:, cut], 1, 1)
    gmiddle_ref[...] = grad_middle
    core = core_ref[0]
    term = joined(ghidden_s)
    split_cores(core, ordered(term, 0), ordered(term, 1), keep_ref, send_ref, 0)
    term = goutput_s[...]
    even = line_ref[0] % 2 == 0
    halves = [[ordered(term, k, lines) for lines in range(2)] for k in range(2)]
    near = [jnp.where(even, a, b) for a, b in halves]
    far = [jnp.where(even, b, a) for a, b in halves]
    split_cores(core, *near, keep_ref, send_ref, FF // 2)
    split_cores(core, *far, keep_ref, send_ref, FF // 4 * 3)


def middle_kernel(
    att_ref, normed_ref, ainverse_ref, gmiddle_ref, proj_ref, again_ref,
    gatt_ref, gproj_ref, vectors_ref,
):
    grad_middle = gmiddle_ref[...]
    attn_normed = normed_ref[...]
    grad_projected = layer_back(grad_middle, attn_normed, ainverse_ref[...], again_ref[...])
    projected_low = grad_projected.astype(BF)
    gatt_ref[...] = dot(proj_ref[...], projected_low, 1, 1).astype(BF)
    vectors_ref[0:1, :] = col_sum(grad_projected) * FACTOR
    vectors_ref[1:2, :] = col_sum(grad_middle * attn_normed) * FACTOR
    vectors_ref[2:3, :] = col_sum(grad_middle) * FACTOR
    grad_proj = dot(att_ref[...], projected_low, 1, 0) * FACTOR
    for c in range(4):
        gproj_ref[pl.ds(c, D, stride=4), :] = grad_proj[:, c * 128 : (c + 1) * 128]


def window_kernel(mixed_ref, gmiddle_ref, qkv_ref, own_ref, down_ref, right_ref, diag_ref):
    window = gmiddle_ref[...] + dot(mixed_ref[...], qkv_ref[...], 1, 1)
    window = window.astype(BF).reshape(WIN, WIN, D)
    own_ref[...] = window[:HALF, :HALF]
    right_ref[...] = window[:HALF, HALF:]
    down_ref[...] = window[HALF:, :HALF]
    diag_ref[...] = window[HALF:, HALF:]


def heads_kernel(
    probs_ref, qunit_ref, kunit_ref, inverse_ref, value_ref, gatt_s,
    logit_ref,
    mixed_ref, sums_ref, wide_s,
    qlow_s, klow_s, gmixed_s,
):
    qlow_s[...] = qunit_ref[...].astype(BF)
    klow_s[...] = kunit_ref[...].astype(BF)

    def head(h, carry):
        at = pl.ds(pl.multiple_of(h * E, E), E)
        kat = pl.ds(pl.multiple_of(h * E + D, E), E)
        vat = pl.ds(pl.multiple_of(h * E + 2 * D, E), E)
        scale = jnp.exp(jnp.minimum(jnp.full((1, T), logit_ref[h], F4), LOG_CAP))
        qlow, klow, gatt = qlow_s[at, :], klow_s[at, :], gatt_s[at, :]
        probs = probs_ref[h]
        grad_probs = dot(value_ref[at, :], gatt, 0, 0)
        gmixed_s[vat, :] = dot(gatt, probs.astype(BF), 1, 1)
        grad_scores = probs * (grad_probs - jnp.sum(probs * grad_probs, 0, keepdims=True))
        cosine = dot(klow, qlow, 0, 0)
        live = jnp.full((1, T), logit_ref[h], F4) < LOG_CAP
        total = jnp.sum(jnp.sum(grad_scores * cosine, 0, keepdims=True), 1, keepdims=True)
        term = jnp.where(live, total * scale * FACTOR, 0.0)
        lane = lax.broadcasted_iota(jnp.int32, (1, T), 1)
        carry = carry + jnp.where(lane == h, term, 0.0)
        grad_cosine = (grad_scores * scale).astype(BF)
        for index, (part, unit_ref, where) in enumerate(
            (
                (dot(klow, grad_cosine, 1, 0), qunit_ref, at),
                (dot(qlow, grad_cosine, 1, 1), kunit_ref, kat),
            )
        ):
            unit = unit_ref[at, :]
            gmixed_s[where, :] = inverse_ref[index, h] * (
                part - unit * jnp.sum(unit * part, 0, keepdims=True)
            )
        wide = None
        for p in range(8):
            first = grad_scores[(15 - p) * 16 : (16 - p) * 16]
            second = grad_scores[(7 - p) * 16 : (8 - p) * 16]
            blank = jnp.zeros((WIN, 128), F4)
            placed = jnp.concatenate(
                [first[:, :128], first[:, 128:] + second[:, :128], second[:, 128:], blank], 1
            )
            if p:
                placed = pltpu.roll(placed, 16 * p, 1)
            wide = placed if wide is None else wide + placed
        wide_s[h] = wide
        return carry

    logits = lax.fori_loop(0, HEADS, head, jnp.zeros((1, T), F4), unroll=2)
    sums_ref[2:3, :] = jnp.concatenate([logits, jnp.zeros((1, D - T), F4)], 1)

    ones = jnp.ones((8, T), F4)
    sums_ref[0:1, :] = dot(ones, gmixed_s[0:D, :], 1, 1, TOP)[:1] * FACTOR
    sums_ref[1:2, :] = dot(ones, gmixed_s[2 * D :, :], 1, 1, TOP)[:1] * FACTOR
    mixed_ref[...] = gmixed_s[...].astype(BF).T


def grads_kernel(x_ref, mixed_ref, gproj_ref, core_ref, keep_ref, send_ref, grads_s):
    mixed = mixed_ref[...]
    for c in range(4):
        cut = slice(c * 384, (c + 1) * 384)
        spread(grads_s, 0, c, dot(x_ref[...], mixed[:, cut], 1, 0) * FACTOR)
    grads = jnp.concatenate([grads_s[0], grads_s[1], grads_s[2], gproj_ref[...]], 1)
    split_cores(core_ref[0], ordered(grads, 0), ordered(grads, 1), keep_ref, send_ref, 0)


def table_kernel(
    entry_ref, exit_ref, squashed_ref, before_ref, wide_s,
    sums_ref, attn_ref, mlp_ref, hsum_ref,
    small_ref,
    small_s,
):
    small_s[0:2, :] = sums_ref[0:2, :]
    small_s[2:5, :] = attn_ref[...]
    small_s[5:8, :] = mlp_ref[...]
    for c in range(0, FF, D):
        small_s[8 + c // D : 9 + c // D, :] = hsum_ref[:, c : c + D]
    small_s[31:32, :] = sums_ref[2:3, :]
    low = low_half((HEADS, LANES))
    even = jnp.zeros((HEADS, LANES), F4)
    odd = jnp.zeros((HEADS, LANES), F4)
    for c in range(WIN):
        part = wide_s[:, c, :]
        even += pltpu.roll(jnp.where(low, part, 0.0), (15 - c) % LANES, 1)
        odd += pltpu.roll(jnp.where(low, 0.0, part), (LANES - 1 - c) % LANES, 1)
    coords, valid = offset_coords()
    squashed = squashed_ref[...]
    table = jnp.concatenate([even, odd], 1) * 16.0 * squashed * (1.0 - squashed) * FACTOR
    table = jnp.where(valid[:1], table, 0.0)
    before = before_ref[...]
    small_s[15:31, :] = dot(table, jnp.maximum(before, 0.0), 1, 1, TOP)
    grad_pos = jnp.where(before > 0.0, dot(exit_ref[...], table, 0, 0, TOP), 0.0)
    small_s[12:15, :] = dot(coords, grad_pos, 1, 1, TOP)[:3]
    small = small_s[...]
    for c in range(4):
        small_ref[pl.ds(c, 32, stride=4), :] = small[:, c * 128 : (c + 1) * 128]


def shape(*dims, dtype=F4):
    return jax.ShapeDtypeStruct(dims, dtype)


def vmem(*dims, dtype=F4):
    return pltpu.VMEM(dims, dtype)


def whole(count, scalar=()):
    return [
        pl.BlockSpec(memory_space=pltpu.SMEM if i in scalar else pltpu.VMEM) for i in range(count)
    ]


def device_index(row, col):
    return (row % 16) * 16 + col % 16


def moved(block, rows, cols):
    route = [
        (device_index(r, c), device_index(r + rows, c + cols)) for r in range(16) for c in range(16)
    ]
    return lax.ppermute(block, ALL, route)


def swapped(block):
    return lax.ppermute(block, "core", [(0, 1), (1, 0)])


def joint(keep, got):
    return (keep.astype(F4) + got.astype(F4)).astype(BF)


def exchanged(blocks, axes):
    return lax.all_to_all(blocks, axes, 0, 0)


def rounds(small, steps):
    for axis, size, step in steps:
        small = small + lax.ppermute(small, axis, [(i, i ^ step) for i in range(size)])
    return small


def across(block):
    return lax.ppermute(block, "z", [(i, i ^ 1) for i in range(8)])


def cost(us):
    return pl.CostEstimate(flops=int(us * 5e8), bytes_accessed=int(us * 2e6), transcendentals=0)


def local(
    tokens, cotangent, regions, qkv_weight, query_bias, value_bias, logit_scale,
    entry_weight, entry_bias, exit_weight, proj_weight, proj_bias, attn_gain, attn_shift,
    hidden_weight, hidden_bias, output_weight, output_bias, mlp_gain,
):
    row = lambda v: v.reshape(1, -1)

    def strip(rows, cols):
        return jnp.concatenate([tokens[:, rows, cols], cotangent[:, rows, cols]], 0)

    head, tail = slice(0, HALF), slice(HALF, WIN)
    down = moved(strip(head, tail), -1, 0)
    right = moved(strip(tail, head), 0, -1)
    diag = moved(strip(head, head), -1, -1)
    exit_turned = exit_weight.T
    wide, squashed, before = pl.pallas_call(
        bias_kernel,
        out_shape=(
            shape(HEADS, WIN, LANES), shape(HEADS, 2 * LANES), shape(D, 2 * LANES),
        ),
        in_specs=whole(3),
        out_specs=tuple(whole(3)),
        scratch_shapes=[vmem(WIN, HEADS, LANES)],
        compiler_params=PARAMS,
        cost_estimate=cost(5),
        name="bias",
    )(entry_weight, row(entry_bias), exit_turned)
    core = lax.axis_index("core").astype(jnp.int32).reshape(1)
    line = lax.axis_index("z").astype(jnp.int32).reshape(1)
    (
        x, probs, qunit, kunit, inverse, value, att, normed, ainverse, gmiddle,
        mlp_vectors, hidden_sum, keep, send,
    ) = pl.pallas_call(
        forward_kernel,
        out_shape=(
            shape(D, T, dtype=BF), shape(HEADS, T, T), shape(D, T), shape(D, T),
            shape(2, HEADS, 1, T), shape(D, T, dtype=BF), shape(D, T, dtype=BF),
            shape(T, D), shape(T, 1), shape(T, D), shape(3, D), shape(1, FF),
            shape(FF, D, dtype=BF), shape(FF, D, dtype=BF),
        ),
        in_specs=whole(22, (10, 20, 21)),
        out_specs=tuple(whole(14)),
        scratch_shapes=[
            vmem(D, T, dtype=BF), vmem(D, T, dtype=BF), vmem(T, FF, dtype=BF), vmem(T, FF),
            vmem(4, FF, 128), vmem(FF, D),
        ],
        compiler_params=PARAMS,
        cost_estimate=cost(17),
        name="forward",
    )(
        tokens, cotangent, down, right, diag, regions, wide,
        qkv_weight, row(query_bias), row(value_bias), logit_scale,
        proj_weight, row(proj_bias), row(attn_gain), row(attn_shift),
        hidden_weight, row(hidden_bias), output_weight, row(output_bias), row(mlp_gain), core, line,
    )
    got = swapped(send)
    grad_att, grad_proj, attn_vectors = pl.pallas_call(
        middle_kernel,
        out_shape=(shape(D, T, dtype=BF), shape(FF, 128), shape(3, D)),
        in_specs=whole(6),
        out_specs=tuple(whole(3)),
        compiler_params=PARAMS,
        cost_estimate=cost(0.5),
        name="middle",
    )(att, normed, ainverse, gmiddle, proj_weight, row(attn_gain))
    early = joint(keep[: FF // 2], got[: FF // 2])
    far = joint(keep[FF // 4 * 3 :], got[FF // 4 * 3 :])
    near = joint(keep[FF // 2 : FF // 4 * 3], got[FF // 2 : FF // 4 * 3])
    early, far, near, grad_att = lax.optimization_barrier((early, far, near, grad_att))
    far = across(far)
    early = exchanged(early.reshape(PLANE, -1, D), PLANE_AXES)
    mixed, token_sums, wide = pl.pallas_call(
        heads_kernel,
        out_shape=(shape(T, 3 * D, dtype=BF), shape(3, D), shape(HEADS, WIN, LANES)),
        in_specs=whole(7, (6,)),
        out_specs=tuple(whole(3)),
        scratch_shapes=[vmem(D, T, dtype=BF), vmem(D, T, dtype=BF), vmem(3 * D, T)],
        compiler_params=PARAMS,
        cost_estimate=cost(0.5),
        name="heads",
    )(probs, qunit, kunit, inverse, value, grad_att, logit_scale)
    small = pl.pallas_call(
        table_kernel,
        out_shape=shape(128, 128),
        in_specs=whole(9),
        out_specs=whole(1)[0],
        scratch_shapes=[vmem(32, D)],
        compiler_params=PARAMS,
        cost_estimate=cost(0.5),
        name="table",
    )(
        entry_weight, exit_turned, squashed, before, wide,
        token_sums, attn_vectors, mlp_vectors, hidden_sum,
    )
    mixed, far, early, small = lax.optimization_barrier((mixed, far, early, small))
    keep, send = pl.pallas_call(
        grads_kernel,
        out_shape=(shape(FF // 2, D, dtype=BF), shape(FF // 2, D, dtype=BF)),
        in_specs=whole(4, (3,)),
        out_specs=tuple(whole(2)),
        scratch_shapes=[vmem(3, FF, 128)],
        compiler_params=PARAMS,
        cost_estimate=cost(0.5),
        name="grads",
    )(x, mixed, grad_proj, core)
    got = swapped(send)
    got, keep, gmiddle = lax.optimization_barrier((got, keep, gmiddle))
    back_own, back_down, back_right, back_diag = pl.pallas_call(
        window_kernel,
        out_shape=tuple(shape(HALF, HALF, D, dtype=BF) for _ in range(4)),
        in_specs=whole(3),
        out_specs=tuple(whole(4)),
        compiler_params=PARAMS,
        cost_estimate=cost(2),
        name="window",
    )(mixed, gmiddle, qkv_weight)
    early = jnp.sum(early.astype(F4), 0)
    late = jnp.concatenate(
        [joint(keep, got).reshape(PLANE, 64, D), joint(near, far).reshape(PLANE, 32, D)], 1
    )
    late = exchanged(late, PLANE_AXES)
    small = rounds(small + swapped(small), (("z", 8, 1), ("z", 8, 2), ("z", 8, 4)))
    plane_steps = (("x", 4, 1), ("x", 4, 2), ("yl", 2, 1), ("yh", 2, 1))
    late, small, back_down, back_right, back_diag = lax.optimization_barrier(
        (late, small, back_down, back_right, back_diag)
    )
    from_above = moved(back_down, 1, 0)
    from_left = moved(back_right, 0, 1)
    from_diag = moved(back_diag, 1, 1)
    small = rounds(small, plane_steps)
    blocks = pl.pallas_call(
        line_kernel,
        out_shape=shape(8, 24, D, dtype=BF),
        in_specs=whole(3, (2,)),
        out_specs=whole(1)[0],
        compiler_params=PARAMS,
        cost_estimate=cost(2),
        name="line",
    )(early, late, line)
    sum_hidden, sum_output, sum_qkv, sum_proj = pl.pallas_call(
        finish_kernel,
        out_shape=(shape(8 * D), shape(8 * D), shape(8 * 384), shape(8 * 128)),
        in_specs=whole(1),
        out_specs=tuple(whole(4)),
        compiler_params=PARAMS,
        cost_estimate=cost(1),
        name="finish",
    )(exchanged(blocks, "z"))
    vectors, hidden_total, logit_total, first, second = pl.pallas_call(
        unpack_kernel,
        out_shape=(shape(8, D), shape(FF), shape(HEADS), shape(3, D), shape(HEADS, D)),
        in_specs=whole(1),
        out_specs=tuple(whole(5)),
        compiler_params=PARAMS,
        cost_estimate=cost(1),
        name="unpack",
    )(small)
    grad_tokens = jnp.concatenate(
        [
            jnp.concatenate([from_diag, from_above], 1),
            jnp.concatenate([from_left, back_own], 1),
        ],
        0,
    )[None]
    return (
        grad_tokens,
        sum_qkv,
        sum_proj,
        sum_hidden,
        sum_output,
        vectors,
        hidden_total,
        logit_total,
        first,
        second.T,
    )


def solution(mesh):
    fine = Mesh(mesh.devices.reshape([n for _, n in AXES]), ALL)
    tile = P(None, ("z", "yh"), ("yl", "x", "core"))
    return jax.shard_map(
        local,
        mesh=fine,
        in_specs=(tile, tile, tile) + (P(),) * 16,
        out_specs=(tile,) + (P(ALL),) * 4 + (P(),) * 5,
        check_vma=False,
    )
```

```python
import math

import jax
import jax.numpy as jnp
from jax import lax
from jax.experimental import pallas as pl
from jax.experimental.pallas import tpu as pltpu
from jax.sharding import Mesh
from jax.sharding import PartitionSpec as P

WIN = 16
HALF = 8
T = 256
D = 512
HEADS = 16
E = 32
FF = 2048
CH = 512
LANES = 512
ALL = ("z", "yh", "yl", "x", "core")
AXES = (("z", 8), ("yh", 2), ("yl", 2), ("x", 4), ("core", 2))
PLANE = 16
DIRECT = 1536
PLANE_AXES = ALL[1:4]
FACTOR = 1.0 / 256.0
LOG_CAP = math.log(100.0)
TOP = lax.Precision.HIGHEST
BF = jnp.bfloat16
F4 = jnp.float32
PARAMS = pltpu.CompilerParams(vmem_limit_bytes=56 * 1024 * 1024)


def dot(a, b, ca, cb, precision=None):
    return lax.dot_general(
        a, b, (((ca,), (cb,)), ((), ())), precision=precision, preferred_element_type=F4
    )


def split(value, count):
    parts = []
    for _ in range(count):
        parts.append(value.astype(BF).astype(F4))
        value = value - parts[-1]
    return parts


def few_rows(a, b):
    a1, a2, a3 = split(a, 3)
    b1, b2, b3 = split(b, 3)
    left = jnp.concatenate([a1, a1, a2, a2, a1, a3], 0).astype(BF)
    right = jnp.concatenate([b1, b2, b1, b2, b3, b1], 0).astype(BF)
    return dot(left, right, 0, 0)


def few_by_wide(a, b, cb):
    rows = a.shape[0]
    left = jnp.concatenate(split(a, 2), 0).astype(BF)
    high, low = [part.astype(BF) for part in split(b, 2)]
    first, second = dot(left, high, 1, cb), dot(left, low, 1, cb)
    return first[:rows] + (first[rows:] + second[:rows])


def layer_stats(inputs):
    center = inputs - jnp.mean(inputs, -1, keepdims=True)
    inverse = lax.rsqrt(jnp.mean(center * center, -1, keepdims=True) + 1e-05)
    return center * inverse, inverse


def layer_back(upstream, normed, inverse, gain):
    scaled = upstream * gain
    inner = (
        scaled
        - jnp.mean(scaled, -1, keepdims=True)
        - normed * jnp.mean(scaled * normed, -1, keepdims=True)
    )
    return inverse * inner


def col_sum(block):
    return jnp.sum(block, 0, keepdims=True)


def offset_coords():
    lane = lax.broadcasted_iota(jnp.int32, (8, 2 * LANES), 1)
    parity = lane // LANES
    rest = lane - parity * LANES
    pair = rest // 32
    first = 2 * pair + parity
    second = rest - pair * 32
    valid = (first < 31) & (second < 31)

    def logged(index):
        u = (index.astype(F4) - 15.0) / 15.0 * 8.0
        size = jnp.log2(jnp.abs(u) + 1.0) / 3.0
        return jnp.where(u > 0.0, size, jnp.where(u < 0.0, -size, 0.0))

    row = lax.broadcasted_iota(jnp.int32, (8, 2 * LANES), 0)
    coords = jnp.where(
        row == 0, logged(first), jnp.where(row == 1, logged(second), jnp.where(row == 2, 1.0, 0.0))
    )
    return coords, valid


def low_half(shape):
    lane = lax.broadcasted_iota(jnp.int32, shape, len(shape) - 1)
    return lane % 32 < 16


def stack_rows(entry, bias):
    return jnp.concatenate([entry, bias, jnp.zeros((5, entry.shape[1]), F4)], 0)


def spread(ref, block, part, term):
    for lane in range(0, term.shape[1], 128):
        ref[block + lane // 128, pl.ds(part, D, stride=4), :] = term[:, lane : lane + 128]


def joined(ref):
    return jnp.concatenate([ref[b] for b in range(4)], 1)


def ordered(term, core):
    parts = term.reshape(8, PLANE, 2, 8, term.shape[1])
    cut = [parts[:, i, core] for i in range(PLANE)]
    return jnp.concatenate(cut, 0).reshape(-1, term.shape[1])


def paired(term, core):
    parts = term.reshape(8, PLANE, 2, 8, term.shape[1])
    cut = [jnp.concatenate([parts[:4, i, core], parts[4:, i, core]], 2) for i in range(PLANE)]
    return jnp.concatenate(cut, 0).reshape(-1, 2 * term.shape[1])


def paired_lines(term, core, lines):
    parts = term.reshape(4, 2, PLANE, 2, 8, term.shape[1])[:, lines]
    cut = [jnp.concatenate([parts[:2, i, core], parts[2:, i, core]], 2) for i in range(PLANE)]
    return jnp.concatenate(cut, 0).reshape(-1, 2 * term.shape[1])


def split_cores(core, first, second, keep_ref, send_ref, start):
    rows = pl.ds(start, first.shape[0])
    keep_ref[rows, :] = jnp.where(core == 0, first, second).astype(BF)
    send_ref[rows, :] = jnp.where(core == 0, second, first).astype(BF)


def line_kernel(early_ref, late_ref, line_ref, out_ref):
    early = early_ref[...]
    late = jnp.sum(late_ref[...].astype(F4), 0)
    half = D // 2
    for z in range(8):
        rows = slice(8 * z, 8 * z + 8)
        spot = 64 + 8 * (z % 4)
        direct = early[spot : spot + 8, z // 4 * half : (z // 4 + 1) * half]
        spot = 64 + 8 * (z // 2 % 2)
        turned = late[spot : spot + 8, z // 4 * half : (z // 4 + 1) * half]
        turned = jnp.where(line_ref[0] % 2 == z % 2, turned, 0.0)
        output = jnp.concatenate([direct, turned], 1)
        out_ref[z] = jnp.concatenate([early[rows], output, late[rows]], 0).astype(BF)


def finish_kernel(blocks_ref, hidden_ref, output_ref, qkv_ref, proj_ref):
    total = jnp.sum(blocks_ref[...].astype(F4), 0)
    for r in range(8):
        hidden_ref[r * D : (r + 1) * D] = total[r]
        output_ref[r * D : (r + 1) * D] = total[8 + r]
        qkv_ref[r * 384 : (r + 1) * 384] = total[16 + r, :384]
        proj_ref[r * 128 : (r + 1) * 128] = total[16 + r, 384:]


def unpack_kernel(small_ref, others_ref, vectors_ref, hidden_ref, logit_ref, first_ref, second_ref):
    rows = [pl.ds(c, 32, stride=4) for c in range(4)]
    total = jnp.concatenate([small_ref[r, :] + others_ref[r, :] for r in rows], 1)
    vectors_ref[...] = total[:8]
    for c in range(4):
        hidden_ref[c * D : (c + 1) * D] = total[8 + c]
    first_ref[...] = total[12:15]
    second_ref[...] = total[15:31]
    logit_ref[...] = total[31, :HEADS]


def bias_kernel(entry_ref, mid_ref, exit_ref, wide_ref, squashed_ref, scratch):
    coords, _ = offset_coords()
    before = few_rows(stack_rows(entry_ref[...], mid_ref[...]), coords)
    hidden = jnp.maximum(before, 0.0)
    squashed = jax.nn.sigmoid(few_by_wide(exit_ref[...], hidden, 0))
    squashed_ref[...] = squashed
    table = 16.0 * squashed
    even, odd = table[:, :LANES], table[:, LANES:]
    low = low_half((HEADS, LANES))
    for c in range(WIN):
        scratch[c] = jnp.where(
            low,
            pltpu.roll(even, (c - 15) % LANES, 1),
            pltpu.roll(odd, (c + 1) % LANES, 1),
        )
    for h in range(HEADS):
        wide_ref[h] = scratch[:, h, :]


def forward_kernel(
    tokens_ref, cotangent_ref, down_ref, right_ref, diag_ref, regions_ref, wide_ref,
    qkv_ref, qbias_ref, vbias_ref, logit_ref,
    proj_ref, pbias_ref, again_ref, ashift_ref,
    hidden_ref, hbias_ref, output_ref, obias_ref, mgain_ref, core_ref, line_ref,
    x_ref, probs_ref, qunit_ref, kunit_ref, inverse_ref, value_ref, att_ref,
    normed_ref, ainverse_ref, gmiddle_ref, vectors_ref, hsum_ref, keep_ref, send_ref,
    qlow_s, klow_s, act_s, slope_s, ghidden_s, goutput_s,
    whidden_s, woutput_s, x_s, probs_s, qunit_s, kunit_s, value_s, att_s, normed_s, gmiddle_s, sems,
):
    loads = [
        pltpu.make_async_copy(hidden_ref, whidden_s, sems.at[0]),
        pltpu.make_async_copy(output_ref, woutput_s, sems.at[1]),
    ]
    for load in loads:
        load.start()
    stores = []

    def store(scratch, ref):
        stores.append(pltpu.make_async_copy(scratch, ref, sems.at[2 + len(stores)]))
        stores[-1].start()

    def assemble(own_ref, i):
        top = jnp.concatenate([own_ref[0, HALF:, HALF:], right_ref[i]], 1)
        bottom = jnp.concatenate([down_ref[i], diag_ref[i]], 1)
        return jnp.concatenate([top, bottom], 0).reshape(T, D)

    x = assemble(tokens_ref, 0)
    x_s[...] = x.T
    store(x_s, x_ref)
    mixed = dot(x, qkv_ref[...], 1, 0)
    q = (mixed[:, :D] + qbias_ref[...]).T
    k = mixed[:, D : 2 * D].T
    value_s[...] = (mixed[:, 2 * D :] + vbias_ref[...]).T.astype(BF)
    for index, (raw, unit_ref, low_s) in enumerate(
        ((q, qunit_s, qlow_s), (k, kunit_s, klow_s))
    ):
        split = raw.reshape(HEADS, E, T)
        inverse = lax.rsqrt(jnp.sum(split * split, 1, keepdims=True) + 1e-06)
        inverse_ref[index] = inverse
        unit = (split * inverse).reshape(D, T)
        unit_ref[...] = unit
        low_s[...] = unit.astype(BF)
    store(qunit_s, qunit_ref)
    store(kunit_s, kunit_ref)
    store(value_s, value_ref)
    own_row = lax.broadcasted_iota(jnp.int32, (WIN, T), 0)
    token = lax.broadcasted_iota(jnp.int32, (WIN, T), 1)
    pick = jnp.where(token % WIN == own_row, 1.0, 0.0).astype(BF)
    by_row = dot(regions_ref[0].astype(F4).astype(BF), pick, 1, 0)
    region_row = col_sum(jnp.where(token // WIN == own_row, by_row, 0.0))
    region_col = jnp.broadcast_to(region_row, (8, T)).T[:, :1]
    allowed = region_col == region_row

    def head(h, carry):
        at = pl.ds(pl.multiple_of(h * E, E), E)
        scale = jnp.exp(jnp.minimum(jnp.full((1, T), logit_ref[h], F4), LOG_CAP))
        cosine = dot(klow_s[at, :], qlow_s[at, :], 0, 0)
        wide = wide_ref[h]
        rolled = [wide] + [pltpu.roll(wide, LANES - 16 * p, 1) for p in range(1, 8)]
        bias = jnp.concatenate(
            [
                rolled[(15 - r) % 8][:, (15 - r) // 8 * 128 : (15 - r) // 8 * 128 + T]
                for r in range(WIN)
            ],
            0,
        )
        logits = jnp.where(allowed, scale * cosine + bias, -1000000000.0)
        powers = jnp.exp(logits - jnp.max(logits, 0, keepdims=True))
        probs = powers / jnp.sum(powers, 0, keepdims=True)
        probs_s[h] = probs
        pltpu.make_async_copy(probs_s.at[h], probs_ref.at[h], sems.at[9]).start()
        att_s[at, :] = dot(value_s[at, :], probs.astype(BF), 1, 0).astype(BF)
        return carry

    lax.fori_loop(0, HEADS, head, 0, unroll=2)

    store(att_s, att_ref)
    projected = dot(att_s[...], proj_ref[...], 0, 0) + pbias_ref[...]
    attn_normed, attn_inverse = layer_stats(projected)
    normed_s[...] = attn_normed
    store(normed_s, normed_ref)
    ainverse_ref[...] = attn_inverse
    middle = x.astype(F4) + (attn_normed * again_ref[...] + ashift_ref[...])
    middle_low = middle.astype(BF)
    for load in loads:
        load.wait()
    emitted = jnp.zeros((T, D), F4)
    for c in range(0, FF, CH):
        cut = slice(c, c + CH)
        before = dot(middle_low, whidden_s[:, cut], 1, 0) + hbias_ref[:, cut]
        cumulative = 0.5 * (1.0 + lax.erf(before * (1.0 / math.sqrt(2.0))))
        density = jnp.exp(-0.5 * before * before) * (1.0 / math.sqrt(2.0 * math.pi))
        slope_s[:, cut] = cumulative + before * density
        act = (before * cumulative).astype(BF)
        act_s[:, cut] = act
        emitted += dot(act, woutput_s[cut, :], 1, 0)
    normed, inverse = layer_stats(emitted + obias_ref[...])
    incoming = assemble(cotangent_ref, 1).astype(F4)
    grad_emitted = layer_back(incoming, normed, inverse, mgain_ref[...])
    emitted_low = grad_emitted.astype(BF)
    vectors_ref[0:1, :] = col_sum(grad_emitted) * FACTOR
    vectors_ref[1:2, :] = col_sum(incoming * normed) * FACTOR
    vectors_ref[2:3, :] = col_sum(incoming) * FACTOR
    grad_middle = incoming
    for c in range(0, FF, CH):
        cut = slice(c, c + CH)
        grad_act = dot(emitted_low, woutput_s[cut, :], 1, 1)
        grad_before = grad_act * slope_s[:, cut]
        hsum_ref[:, cut] = col_sum(grad_before) * FACTOR
        before_low = grad_before.astype(BF)
        goutput_s[cut, :] = dot(act_s[:, cut], emitted_low, 0, 0) * FACTOR
        spread(ghidden_s, 0, c // CH, dot(middle_low, before_low, 0, 0) * FACTOR)
        grad_middle += dot(before_low, whidden_s[:, cut], 1, 1)
    gmiddle_s[...] = grad_middle
    store(gmiddle_s, gmiddle_ref)
    core = core_ref[0]
    term = joined(ghidden_s)
    split_cores(core, ordered(term, 0), ordered(term, 1), keep_ref, send_ref, 0)
    term = goutput_s[...]
    even = line_ref[0] % 2 == 0
    half = D // 2
    direct, turned = term[:, :half], term[:, half:]
    split_cores(core, paired(direct, 0), paired(direct, 1), keep_ref, send_ref, FF // 2)
    halves = [[paired_lines(turned, k, lines) for lines in range(2)] for k in range(2)]
    near = [jnp.where(even, a, b) for a, b in halves]
    far = [jnp.where(even, b, a) for a, b in halves]
    split_cores(core, *near, keep_ref, send_ref, DIRECT)
    split_cores(core, *far, keep_ref, send_ref, DIRECT + 256)
    pltpu.make_async_copy(probs_s, probs_ref, sems.at[9]).wait()
    for done in stores:
        done.wait()


def middle_kernel(
    att_ref, normed_ref, ainverse_ref, gmiddle_ref, proj_ref, again_ref,
    gatt_ref, gproj_ref, vectors_ref,
):
    grad_middle = gmiddle_ref[...]
    attn_normed = normed_ref[...]
    grad_projected = layer_back(grad_middle, attn_normed, ainverse_ref[...], again_ref[...])
    projected_low = grad_projected.astype(BF)
    gatt_ref[...] = dot(proj_ref[...], projected_low, 1, 1).astype(BF)
    vectors_ref[0:1, :] = col_sum(grad_projected) * FACTOR
    vectors_ref[1:2, :] = col_sum(grad_middle * attn_normed) * FACTOR
    vectors_ref[2:3, :] = col_sum(grad_middle) * FACTOR
    grad_proj = dot(att_ref[...], projected_low, 1, 0) * FACTOR
    for c in range(4):
        gproj_ref[pl.ds(c, D, stride=4), :] = grad_proj[:, c * 128 : (c + 1) * 128]


def window_kernel(mixed_ref, gmiddle_ref, qkv_ref, own_ref, down_ref, right_ref, diag_ref):
    window = gmiddle_ref[...] + dot(mixed_ref[...], qkv_ref[...], 1, 1)
    window = window.astype(BF).reshape(WIN, WIN, D)
    own_ref[...] = window[:HALF, :HALF]
    right_ref[...] = window[:HALF, HALF:]
    down_ref[...] = window[HALF:, :HALF]
    diag_ref[...] = window[HALF:, HALF:]


def heads_kernel(
    probs_ref, qunit_ref, kunit_ref, inverse_ref, value_ref, gatt_s,
    logit_ref,
    mixed_ref, sums_ref, wide_s,
    qlow_s, klow_s, gmixed_s,
):
    qlow_s[...] = qunit_ref[...].astype(BF)
    klow_s[...] = kunit_ref[...].astype(BF)

    def head(h, carry):
        at = pl.ds(pl.multiple_of(h * E, E), E)
        kat = pl.ds(pl.multiple_of(h * E + D, E), E)
        vat = pl.ds(pl.multiple_of(h * E + 2 * D, E), E)
        scale = jnp.exp(jnp.minimum(jnp.full((1, T), logit_ref[h], F4), LOG_CAP))
        qlow, klow, gatt = qlow_s[at, :], klow_s[at, :], gatt_s[at, :]
        probs = probs_ref[h]
        grad_probs = dot(value_ref[at, :], gatt, 0, 0)
        gmixed_s[vat, :] = dot(gatt, probs.astype(BF), 1, 1)
        grad_scores = probs * (grad_probs - jnp.sum(probs * grad_probs, 0, keepdims=True))
        cosine = dot(klow, qlow, 0, 0)
        live = jnp.full((1, T), logit_ref[h], F4) < LOG_CAP
        total = jnp.sum(jnp.sum(grad_scores * cosine, 0, keepdims=True), 1, keepdims=True)
        term = jnp.where(live, total * scale * FACTOR, 0.0)
        lane = lax.broadcasted_iota(jnp.int32, (1, T), 1)
        carry = carry + jnp.where(lane == h, term, 0.0)
        grad_cosine = (grad_scores * scale).astype(BF)
        for index, (part, unit_ref, where) in enumerate(
            (
                (dot(klow, grad_cosine, 1, 0), qunit_ref, at),
                (dot(qlow, grad_cosine, 1, 1), kunit_ref, kat),
            )
        ):
            unit = unit_ref[at, :]
            gmixed_s[where, :] = inverse_ref[index, h] * (
                part - unit * jnp.sum(unit * part, 0, keepdims=True)
            )
        wide = None
        for p in range(8):
            first = grad_scores[(15 - p) * 16 : (16 - p) * 16]
            second = grad_scores[(7 - p) * 16 : (8 - p) * 16]
            blank = jnp.zeros((WIN, 128), F4)
            placed = jnp.concatenate(
                [first[:, :128], first[:, 128:] + second[:, :128], second[:, 128:], blank], 1
            )
            if p:
                placed = pltpu.roll(placed, 16 * p, 1)
            wide = placed if wide is None else wide + placed
        wide_s[h] = wide
        return carry

    logits = lax.fori_loop(0, HEADS, head, jnp.zeros((1, T), F4), unroll=2)
    sums_ref[2:3, :] = jnp.concatenate([logits, jnp.zeros((1, D - T), F4)], 1)

    ones = jnp.ones((8, T), F4)
    sums_ref[0:1, :] = few_by_wide(ones, gmixed_s[0:D, :], 1)[:1] * FACTOR
    sums_ref[1:2, :] = few_by_wide(ones, gmixed_s[2 * D :, :], 1)[:1] * FACTOR
    mixed_ref[...] = gmixed_s[...].astype(BF).T


def grads_kernel(x_ref, mixed_ref, gproj_ref, core_ref, keep_ref, send_ref, grads_s):
    mixed = mixed_ref[...]
    for c in range(4):
        cut = slice(c * 384, (c + 1) * 384)
        spread(grads_s, 0, c, dot(x_ref[...], mixed[:, cut], 1, 0) * FACTOR)
    grads = jnp.concatenate([grads_s[0], grads_s[1], grads_s[2], gproj_ref[...]], 1)
    split_cores(core_ref[0], ordered(grads, 0), ordered(grads, 1), keep_ref, send_ref, 0)


def table_kernel(
    entry_ref, mid_ref, exit_ref, squashed_ref, wide_s,
    sums_ref, attn_ref, mlp_ref, hsum_ref,
    small_ref,
    small_s,
):
    small_s[0:2, :] = sums_ref[0:2, :]
    small_s[2:5, :] = attn_ref[...]
    small_s[5:8, :] = mlp_ref[...]
    for c in range(0, FF, D):
        small_s[8 + c // D : 9 + c // D, :] = hsum_ref[:, c : c + D]
    small_s[31:32, :] = sums_ref[2:3, :]
    low = low_half((HEADS, LANES))
    even = jnp.zeros((HEADS, LANES), F4)
    odd = jnp.zeros((HEADS, LANES), F4)
    for c in range(WIN):
        part = wide_s[:, c, :]
        even += pltpu.roll(jnp.where(low, part, 0.0), (15 - c) % LANES, 1)
        odd += pltpu.roll(jnp.where(low, 0.0, part), (LANES - 1 - c) % LANES, 1)
    coords, valid = offset_coords()
    squashed = squashed_ref[...]
    table = jnp.concatenate([even, odd], 1) * 16.0 * squashed * (1.0 - squashed) * FACTOR
    table = jnp.where(valid[:1], table, 0.0)
    before = few_rows(stack_rows(entry_ref[...], mid_ref[...]), coords)
    small_s[15:31, :] = few_by_wide(table, jnp.maximum(before, 0.0), 1)
    grad_pos = jnp.where(before > 0.0, few_rows(exit_ref[...], table), 0.0)
    small_s[12:15, :] = few_by_wide(coords, grad_pos, 1)[:3]
    small = small_s[...]
    for c in range(4):
        small_ref[pl.ds(c, 32, stride=4), :] = small[:, c * 128 : (c + 1) * 128]


def shape(*dims, dtype=F4):
    return jax.ShapeDtypeStruct(dims, dtype)


def vmem(*dims, dtype=F4):
    return pltpu.VMEM(dims, dtype)


def whole(count, scalar=(), far=()):
    def space(i):
        return pltpu.SMEM if i in scalar else pl.ANY if i in far else pltpu.VMEM

    return [pl.BlockSpec(memory_space=space(i)) for i in range(count)]


def device_index(row, col):
    return (row % 16) * 16 + col % 16


def moved(block, rows, cols):
    route = [
        (device_index(r, c), device_index(r + rows, c + cols)) for r in range(16) for c in range(16)
    ]
    return lax.ppermute(block, ALL, route)


def swapped(block):
    return lax.ppermute(block, "core", [(0, 1), (1, 0)])


def joint(keep, got):
    return (keep.astype(F4) + got.astype(F4)).astype(BF)


def exchanged(blocks, axes):
    return lax.all_to_all(blocks, axes, 0, 0)


def rounds(small, steps):
    for axis, size, step in steps:
        small = small + lax.ppermute(small, axis, [(i, i ^ step) for i in range(size)])
    return small


def across(block):
    return lax.ppermute(block, "z", [(i, i ^ 1) for i in range(8)])


def cost(us):
    return pl.CostEstimate(flops=int(us * 5e8), bytes_accessed=int(us * 2e6), transcendentals=0)


def local(
    tokens, cotangent, regions, qkv_weight, query_bias, value_bias, logit_scale,
    entry_weight, entry_bias, exit_weight, proj_weight, proj_bias, attn_gain, attn_shift,
    hidden_weight, hidden_bias, output_weight, output_bias, mlp_gain,
):
    row = lambda v: v.reshape(1, -1)

    def strip(rows, cols):
        return jnp.concatenate([tokens[:, rows, cols], cotangent[:, rows, cols]], 0)

    head, tail = slice(0, HALF), slice(HALF, WIN)
    down = moved(strip(head, tail), -1, 0)
    right = moved(strip(tail, head), 0, -1)
    diag = moved(strip(head, head), -1, -1)
    exit_turned = exit_weight.T
    wide, squashed = pl.pallas_call(
        bias_kernel,
        out_shape=(
            shape(HEADS, WIN, LANES), shape(HEADS, 2 * LANES),
        ),
        in_specs=whole(3),
        out_specs=tuple(whole(2)),
        scratch_shapes=[vmem(WIN, HEADS, LANES)],
        compiler_params=PARAMS,
        cost_estimate=cost(5),
        name="bias",
    )(entry_weight, row(entry_bias), exit_turned)
    core = lax.axis_index("core").astype(jnp.int32).reshape(1)
    line = lax.axis_index("z").astype(jnp.int32).reshape(1)
    (
        x, probs, qunit, kunit, inverse, value, att, normed, ainverse, gmiddle,
        mlp_vectors, hidden_sum, keep, send,
    ) = pl.pallas_call(
        forward_kernel,
        out_shape=(
            shape(D, T, dtype=BF), shape(HEADS, T, T), shape(D, T), shape(D, T),
            shape(2, HEADS, 1, T), shape(D, T, dtype=BF), shape(D, T, dtype=BF),
            shape(T, D), shape(T, 1), shape(T, D), shape(3, D), shape(1, FF),
            shape(FF, D, dtype=BF), shape(FF, D, dtype=BF),
        ),
        in_specs=whole(22, (10, 20, 21), (15, 17)),
        out_specs=tuple(whole(14, (), (0, 1, 2, 3, 5, 6, 7, 9))),
        scratch_shapes=[
            vmem(D, T, dtype=BF), vmem(D, T, dtype=BF), vmem(T, FF, dtype=BF), vmem(T, FF),
            vmem(4, FF, 128), vmem(FF, D),
            vmem(D, FF, dtype=BF), vmem(FF, D, dtype=BF), vmem(D, T, dtype=BF),
            vmem(HEADS, T, T), vmem(D, T), vmem(D, T), vmem(D, T, dtype=BF),
            vmem(D, T, dtype=BF), vmem(T, D), vmem(T, D), pltpu.SemaphoreType.DMA((10,)),
        ],
        compiler_params=PARAMS,
        cost_estimate=cost(17),
        name="forward",
    )(
        tokens, cotangent, down, right, diag, regions, wide,
        qkv_weight, row(query_bias), row(value_bias), logit_scale,
        proj_weight, row(proj_bias), row(attn_gain), row(attn_shift),
        hidden_weight, row(hidden_bias), output_weight, row(output_bias), row(mlp_gain), core, line,
    )
    got = swapped(send)
    grad_att, grad_proj, attn_vectors = pl.pallas_call(
        middle_kernel,
        out_shape=(shape(D, T, dtype=BF), shape(FF, 128), shape(3, D)),
        in_specs=whole(6),
        out_specs=tuple(whole(3)),
        compiler_params=PARAMS,
        cost_estimate=cost(0.5),
        name="middle",
    )(att, normed, ainverse, gmiddle, proj_weight, row(attn_gain))
    early = jnp.concatenate(
        [
            joint(keep[:1024], got[:1024]).reshape(PLANE, 64, D),
            joint(keep[1024:DIRECT], got[1024:DIRECT]).reshape(PLANE, 32, D),
        ],
        1,
    )
    far = joint(keep[DIRECT + 256 :], got[DIRECT + 256 :])
    near = joint(keep[DIRECT : DIRECT + 256], got[DIRECT : DIRECT + 256])
    early, far, near, grad_att = lax.optimization_barrier((early, far, near, grad_att))
    far = across(far)
    early = exchanged(early, PLANE_AXES)
    mixed, token_sums, wide = pl.pallas_call(
        heads_kernel,
        out_shape=(shape(T, 3 * D, dtype=BF), shape(3, D), shape(HEADS, WIN, LANES)),
        in_specs=whole(7, (6,)),
        out_specs=tuple(whole(3)),
        scratch_shapes=[vmem(D, T, dtype=BF), vmem(D, T, dtype=BF), vmem(3 * D, T)],
        compiler_params=PARAMS,
        cost_estimate=cost(0.5),
        name="heads",
    )(probs, qunit, kunit, inverse, value, grad_att, logit_scale)
    small = pl.pallas_call(
        table_kernel,
        out_shape=shape(128, 128),
        in_specs=whole(9),
        out_specs=whole(1)[0],
        scratch_shapes=[vmem(32, D)],
        compiler_params=PARAMS,
        cost_estimate=cost(0.5),
        name="table",
    )(
        entry_weight, row(entry_bias), exit_turned, squashed, wide,
        token_sums, attn_vectors, mlp_vectors, hidden_sum,
    )
    mixed, far, small = lax.optimization_barrier((mixed, far, small))
    keep, send = pl.pallas_call(
        grads_kernel,
        out_shape=(shape(FF // 2, D, dtype=BF), shape(FF // 2, D, dtype=BF)),
        in_specs=whole(4, (3,)),
        out_specs=tuple(whole(2)),
        scratch_shapes=[vmem(3, FF, 128)],
        compiler_params=PARAMS,
        cost_estimate=cost(0.5),
        name="grads",
    )(x, mixed, grad_proj, core)
    got = swapped(send)
    small = small + swapped(small)
    mixed, small = lax.optimization_barrier((mixed, small))
    small = rounds(small, (("z", 8, 1),))
    back_own, back_down, back_right, back_diag = pl.pallas_call(
        window_kernel,
        out_shape=tuple(shape(HALF, HALF, D, dtype=BF) for _ in range(4)),
        in_specs=whole(3),
        out_specs=tuple(whole(4)),
        compiler_params=PARAMS,
        cost_estimate=cost(2),
        name="window",
    )(mixed, gmiddle, qkv_weight)
    got, keep, early, small, back_own, back_down, back_right, back_diag = lax.optimization_barrier(
        (got, keep, early, small, back_own, back_down, back_right, back_diag)
    )
    early = jnp.sum(early.astype(F4), 0)
    late = jnp.concatenate(
        [joint(keep, got).reshape(PLANE, 64, D), joint(near, far).reshape(PLANE, 16, D)], 1
    )
    late = exchanged(late, PLANE_AXES)
    small = rounds(small, (("z", 8, 2), ("z", 8, 4), ("x", 4, 1)))
    from_above = moved(back_down, 1, 0)
    from_left = moved(back_right, 0, 1)
    from_diag = moved(back_diag, 1, 1)
    grad_tokens = jnp.concatenate(
        [
            jnp.concatenate([from_diag, from_above], 1),
            jnp.concatenate([from_left, back_own], 1),
        ],
        0,
    )[None]
    late, small, grad_tokens = lax.optimization_barrier((late, small, grad_tokens))
    small = rounds(small, (("x", 4, 2), ("yl", 2, 1)))
    blocks = pl.pallas_call(
        line_kernel,
        out_shape=shape(8, 24, D, dtype=BF),
        in_specs=whole(3, (2,)),
        out_specs=whole(1)[0],
        compiler_params=PARAMS,
        cost_estimate=cost(2),
        name="line",
    )(early, late, line)
    sum_hidden, sum_output, sum_qkv, sum_proj = pl.pallas_call(
        finish_kernel,
        out_shape=(shape(8 * D), shape(8 * D), shape(8 * 384), shape(8 * 128)),
        in_specs=whole(1),
        out_specs=tuple(whole(4)),
        compiler_params=PARAMS,
        cost_estimate=cost(1),
        name="finish",
    )(exchanged(blocks, "z"))
    small, sum_hidden, sum_output, sum_qkv, sum_proj = lax.optimization_barrier(
        (small, sum_hidden, sum_output, sum_qkv, sum_proj)
    )
    others = lax.ppermute(small, "yh", [(0, 1), (1, 0)])
    vectors, hidden_total, logit_total, first, second = pl.pallas_call(
        unpack_kernel,
        out_shape=(shape(8, D), shape(FF), shape(HEADS), shape(3, D), shape(HEADS, D)),
        in_specs=whole(2),
        out_specs=tuple(whole(5)),
        compiler_params=PARAMS,
        cost_estimate=cost(1),
        name="unpack",
    )(small, others)
    return (
        grad_tokens,
        sum_qkv,
        sum_proj,
        sum_hidden,
        sum_output,
        vectors,
        hidden_total,
        logit_total,
        first,
        second.T,
    )


def solution(mesh):
    fine = Mesh(mesh.devices.reshape([n for _, n in AXES]), ALL)
    tile = P(None, ("z", "yh"), ("yl", "x", "core"))
    return jax.shard_map(
        local,
        mesh=fine,
        in_specs=(tile, tile, tile) + (P(),) * 16,
        out_specs=(tile,) + (P(ALL),) * 4 + (P(),) * 5,
        check_vma=False,
    )
```

```python
import math

import jax
import jax.numpy as jnp
from jax import lax
from jax.experimental import pallas as pl
from jax.experimental.pallas import tpu as pltpu
from jax.sharding import Mesh
from jax.sharding import PartitionSpec as P

WIN = 16
HALF = 8
T = 256
D = 512
HEADS = 16
E = 32
FF = 2048
CH = 512
LANES = 512
ALL = ("z", "yh", "yl", "x", "core")
AXES = (("z", 8), ("yh", 2), ("yl", 2), ("x", 4), ("core", 2))
PLANE = 16
DIRECT = 1536
PLANE_AXES = ALL[1:4]
FACTOR = 1.0 / 256.0
LOG_CAP = math.log(100.0)
TOP = lax.Precision.HIGHEST
BF = jnp.bfloat16
F4 = jnp.float32
PARAMS = pltpu.CompilerParams(vmem_limit_bytes=56 * 1024 * 1024)


def dot(a, b, ca, cb, precision=None):
    return lax.dot_general(
        a, b, (((ca,), (cb,)), ((), ())), precision=precision, preferred_element_type=F4
    )


def split(value, count):
    parts = []
    for _ in range(count):
        parts.append(value.astype(BF).astype(F4))
        value = value - parts[-1]
    return parts


def few_rows(a, b):
    a1, a2, a3 = split(a, 3)
    b1, b2, b3 = split(b, 3)
    left = jnp.concatenate([a1, a1, a2, a2, a1, a3], 0).astype(BF)
    right = jnp.concatenate([b1, b2, b1, b2, b3, b1], 0).astype(BF)
    return dot(left, right, 0, 0)


def few_by_wide(a, b, cb):
    rows = a.shape[0]
    left = jnp.concatenate(split(a, 2), 0).astype(BF)
    high, low = [part.astype(BF) for part in split(b, 2)]
    first, second = dot(left, high, 1, cb), dot(left, low, 1, cb)
    return first[:rows] + (first[rows:] + second[:rows])


def layer_stats(inputs):
    center = inputs - jnp.mean(inputs, -1, keepdims=True)
    inverse = lax.rsqrt(jnp.mean(center * center, -1, keepdims=True) + 1e-05)
    return center * inverse, inverse


def layer_back(upstream, normed, inverse, gain):
    scaled = upstream * gain
    inner = (
        scaled
        - jnp.mean(scaled, -1, keepdims=True)
        - normed * jnp.mean(scaled * normed, -1, keepdims=True)
    )
    return inverse * inner


def col_sum(block):
    return jnp.sum(block, 0, keepdims=True)


def offset_coords():
    lane = lax.broadcasted_iota(jnp.int32, (8, 2 * LANES), 1)
    parity = lane // LANES
    rest = lane - parity * LANES
    pair = rest // 32
    first = 2 * pair + parity
    second = rest - pair * 32
    valid = (first < 31) & (second < 31)

    def logged(index):
        u = (index.astype(F4) - 15.0) / 15.0 * 8.0
        size = jnp.log2(jnp.abs(u) + 1.0) / 3.0
        return jnp.where(u > 0.0, size, jnp.where(u < 0.0, -size, 0.0))

    row = lax.broadcasted_iota(jnp.int32, (8, 2 * LANES), 0)
    coords = jnp.where(
        row == 0, logged(first), jnp.where(row == 1, logged(second), jnp.where(row == 2, 1.0, 0.0))
    )
    return coords, valid


def low_half(shape):
    lane = lax.broadcasted_iota(jnp.int32, shape, len(shape) - 1)
    return lane % 32 < 16


def stack_rows(entry, bias):
    return jnp.concatenate([entry, bias, jnp.zeros((5, entry.shape[1]), F4)], 0)


def spread(ref, block, part, term):
    for lane in range(0, term.shape[1], 128):
        ref[block + lane // 128, pl.ds(part, D, stride=4), :] = term[:, lane : lane + 128]


def joined(ref):
    return jnp.concatenate([ref[b] for b in range(4)], 1)


def ordered(term, core):
    parts = term.reshape(8, PLANE, 2, 8, term.shape[1])
    cut = [parts[:, i, core] for i in range(PLANE)]
    return jnp.concatenate(cut, 0).reshape(-1, term.shape[1])


def paired(term, core):
    parts = term.reshape(8, PLANE, 2, 8, term.shape[1])
    cut = [jnp.concatenate([parts[:4, i, core], parts[4:, i, core]], 2) for i in range(PLANE)]
    return jnp.concatenate(cut, 0).reshape(-1, 2 * term.shape[1])


def paired_lines(term, core, lines):
    parts = term.reshape(4, 2, PLANE, 2, 8, term.shape[1])[:, lines]
    cut = [jnp.concatenate([parts[:2, i, core], parts[2:, i, core]], 2) for i in range(PLANE)]
    return jnp.concatenate(cut, 0).reshape(-1, 2 * term.shape[1])


def split_cores(core, first, second, keep_ref, send_ref, start):
    rows = pl.ds(start, first.shape[0])
    keep_ref[rows, :] = jnp.where(core == 0, first, second).astype(BF)
    send_ref[rows, :] = jnp.where(core == 0, second, first).astype(BF)


def line_kernel(early_ref, late_ref, line_ref, out_ref):
    early = early_ref[...]
    late = jnp.sum(late_ref[...].astype(F4), 0)
    half = D // 2
    for z in range(8):
        rows = slice(8 * z, 8 * z + 8)
        spot = 64 + 8 * (z % 4)
        direct = early[spot : spot + 8, z // 4 * half : (z // 4 + 1) * half]
        spot = 64 + 8 * (z // 2 % 2)
        turned = late[spot : spot + 8, z // 4 * half : (z // 4 + 1) * half]
        turned = jnp.where(line_ref[0] % 2 == z % 2, turned, 0.0)
        output = jnp.concatenate([direct, turned], 1)
        out_ref[z] = jnp.concatenate([early[rows], output, late[rows]], 0).astype(BF)


def finish_kernel(
    blocks_ref, small_ref, others_ref,
    hidden_ref, output_ref, qkv_ref, proj_ref,
    vectors_ref, hbias_ref, logit_ref, first_ref, second_ref,
):
    total = jnp.sum(blocks_ref[...].astype(F4), 0)
    for r in range(8):
        hidden_ref[r * D : (r + 1) * D] = total[r]
        output_ref[r * D : (r + 1) * D] = total[8 + r]
        qkv_ref[r * 384 : (r + 1) * 384] = total[16 + r, :384]
        proj_ref[r * 128 : (r + 1) * 128] = total[16 + r, 384:]
    rows = [pl.ds(c, 32, stride=4) for c in range(4)]
    total = jnp.concatenate([small_ref[r, :] + others_ref[r, :] for r in rows], 1)
    vectors_ref[...] = total[:8]
    for c in range(4):
        hbias_ref[c * D : (c + 1) * D] = total[8 + c]
    first_ref[...] = total[12:15]
    second_ref[...] = total[15:31]
    logit_ref[...] = total[31, :HEADS]


def bias_kernel(entry_ref, mid_ref, exit_ref, wide_ref, squashed_ref, scratch):
    coords, _ = offset_coords()
    before = few_rows(stack_rows(entry_ref[...], mid_ref[...]), coords)
    hidden = jnp.maximum(before, 0.0)
    squashed = jax.nn.sigmoid(few_by_wide(exit_ref[...], hidden, 0))
    squashed_ref[...] = squashed
    table = 16.0 * squashed
    even, odd = table[:, :LANES], table[:, LANES:]
    low = low_half((HEADS, LANES))
    for c in range(WIN):
        scratch[c] = jnp.where(
            low,
            pltpu.roll(even, (c - 15) % LANES, 1),
            pltpu.roll(odd, (c + 1) % LANES, 1),
        )
    for h in range(HEADS):
        wide_ref[h] = scratch[:, h, :]


def forward_kernel(
    tokens_ref, cotangent_ref, down_ref, right_ref, diag_ref, regions_ref, wide_ref,
    qkv_ref, qbias_ref, vbias_ref, logit_ref,
    proj_ref, pbias_ref, again_ref, ashift_ref,
    hidden_ref, hbias_ref, output_ref, obias_ref, mgain_ref, core_ref, line_ref,
    x_ref, probs_ref, qunit_ref, kunit_ref, inverse_ref, value_ref, att_ref,
    normed_ref, ainverse_ref, gmiddle_ref, vectors_ref, hsum_ref, keep_ref, send_ref,
    qlow_s, klow_s, act_s, slope_s, ghidden_s, goutput_s,
    whidden_s, woutput_s, x_s, probs_s, qunit_s, kunit_s, value_s, att_s, normed_s, gmiddle_s, sems,
):
    loads = [
        pltpu.make_async_copy(hidden_ref, whidden_s, sems.at[0]),
        pltpu.make_async_copy(output_ref, woutput_s, sems.at[1]),
    ]
    for load in loads:
        load.start()
    stores = []

    def store(scratch, ref):
        stores.append(pltpu.make_async_copy(scratch, ref, sems.at[2 + len(stores)]))
        stores[-1].start()

    def assemble(own_ref, i):
        top = jnp.concatenate([own_ref[0, HALF:, HALF:], right_ref[i]], 1)
        bottom = jnp.concatenate([down_ref[i], diag_ref[i]], 1)
        return jnp.concatenate([top, bottom], 0).reshape(T, D)

    x = assemble(tokens_ref, 0)
    x_s[...] = x.T
    store(x_s, x_ref)
    mixed = dot(x, qkv_ref[...], 1, 0)
    q = (mixed[:, :D] + qbias_ref[...]).T
    k = mixed[:, D : 2 * D].T
    value_s[...] = (mixed[:, 2 * D :] + vbias_ref[...]).T.astype(BF)
    for index, (raw, unit_ref, low_s) in enumerate(
        ((q, qunit_s, qlow_s), (k, kunit_s, klow_s))
    ):
        split = raw.reshape(HEADS, E, T)
        inverse = lax.rsqrt(jnp.sum(split * split, 1, keepdims=True) + 1e-06)
        inverse_ref[index] = inverse
        unit = (split * inverse).reshape(D, T)
        unit_ref[...] = unit
        low_s[...] = unit.astype(BF)
    store(qunit_s, qunit_ref)
    store(kunit_s, kunit_ref)
    store(value_s, value_ref)
    own_row = lax.broadcasted_iota(jnp.int32, (WIN, T), 0)
    token = lax.broadcasted_iota(jnp.int32, (WIN, T), 1)
    pick = jnp.where(token % WIN == own_row, 1.0, 0.0).astype(BF)
    by_row = dot(regions_ref[0].astype(F4).astype(BF), pick, 1, 0)
    region_row = col_sum(jnp.where(token // WIN == own_row, by_row, 0.0))
    region_col = jnp.broadcast_to(region_row, (8, T)).T[:, :1]
    allowed = region_col == region_row

    def head(h, carry):
        at = pl.ds(pl.multiple_of(h * E, E), E)
        scale = jnp.exp(jnp.minimum(jnp.full((1, T), logit_ref[h], F4), LOG_CAP))
        cosine = dot(klow_s[at, :], qlow_s[at, :], 0, 0)
        wide = wide_ref[h]
        rolled = [wide] + [pltpu.roll(wide, LANES - 16 * p, 1) for p in range(1, 8)]
        bias = jnp.concatenate(
            [
                rolled[(15 - r) % 8][:, (15 - r) // 8 * 128 : (15 - r) // 8 * 128 + T]
                for r in range(WIN)
            ],
            0,
        )
        logits = jnp.where(allowed, scale * cosine + bias, -1000000000.0)
        powers = jnp.exp(logits - jnp.max(logits, 0, keepdims=True))
        probs = powers * (1.0 / jnp.sum(powers, 0, keepdims=True))
        probs_s[h] = probs
        pltpu.make_async_copy(probs_s.at[h], probs_ref.at[h], sems.at[9]).start()
        att_s[at, :] = dot(value_s[at, :], probs.astype(BF), 1, 0).astype(BF)
        return carry

    lax.fori_loop(0, HEADS, head, 0, unroll=4)

    store(att_s, att_ref)
    projected = dot(att_s[...], proj_ref[...], 0, 0) + pbias_ref[...]
    attn_normed, attn_inverse = layer_stats(projected)
    normed_s[...] = attn_normed
    store(normed_s, normed_ref)
    ainverse_ref[...] = attn_inverse
    middle = x.astype(F4) + (attn_normed * again_ref[...] + ashift_ref[...])
    middle_low = middle.astype(BF)
    for load in loads:
        load.wait()
    emitted = jnp.zeros((T, D), F4)
    for c in range(0, FF, CH):
        cut = slice(c, c + CH)
        before = dot(middle_low, whidden_s[:, cut], 1, 0) + hbias_ref[:, cut]
        cumulative = 0.5 * (1.0 + lax.erf(before * (1.0 / math.sqrt(2.0))))
        density = jnp.exp(-0.5 * before * before) * (1.0 / math.sqrt(2.0 * math.pi))
        slope_s[:, cut] = cumulative + before * density
        act = (before * cumulative).astype(BF)
        act_s[:, cut] = act
        emitted += dot(act, woutput_s[cut, :], 1, 0)
    normed, inverse = layer_stats(emitted + obias_ref[...])
    incoming = assemble(cotangent_ref, 1).astype(F4)
    grad_emitted = layer_back(incoming, normed, inverse, mgain_ref[...])
    emitted_low = grad_emitted.astype(BF)
    vectors_ref[0:1, :] = col_sum(grad_emitted) * FACTOR
    vectors_ref[1:2, :] = col_sum(incoming * normed) * FACTOR
    vectors_ref[2:3, :] = col_sum(incoming) * FACTOR
    grad_middle = incoming
    for c in range(0, FF, CH):
        cut = slice(c, c + CH)
        grad_act = dot(emitted_low, woutput_s[cut, :], 1, 1)
        grad_before = grad_act * slope_s[:, cut]
        hsum_ref[:, cut] = col_sum(grad_before) * FACTOR
        before_low = grad_before.astype(BF)
        goutput_s[cut, :] = dot(act_s[:, cut], emitted_low, 0, 0) * FACTOR
        spread(ghidden_s, 0, c // CH, dot(middle_low, before_low, 0, 0) * FACTOR)
        grad_middle += dot(before_low, whidden_s[:, cut], 1, 1)
    gmiddle_s[...] = grad_middle
    store(gmiddle_s, gmiddle_ref)
    core = core_ref[0]
    term = joined(ghidden_s)
    split_cores(core, ordered(term, 0), ordered(term, 1), keep_ref, send_ref, 0)
    term = goutput_s[...]
    even = line_ref[0] % 2 == 0
    half = D // 2
    direct, turned = term[:, :half], term[:, half:]
    split_cores(core, paired(direct, 0), paired(direct, 1), keep_ref, send_ref, FF // 2)
    halves = [[paired_lines(turned, k, lines) for lines in range(2)] for k in range(2)]
    near = [jnp.where(even, a, b) for a, b in halves]
    far = [jnp.where(even, b, a) for a, b in halves]
    split_cores(core, *near, keep_ref, send_ref, DIRECT)
    split_cores(core, *far, keep_ref, send_ref, DIRECT + 256)
    pltpu.make_async_copy(probs_s, probs_ref, sems.at[9]).wait()
    for done in stores:
        done.wait()


def middle_kernel(
    att_ref, normed_ref, ainverse_ref, gmiddle_ref, proj_ref, again_ref,
    gatt_ref, gproj_ref, vectors_ref,
):
    grad_middle = gmiddle_ref[...]
    attn_normed = normed_ref[...]
    grad_projected = layer_back(grad_middle, attn_normed, ainverse_ref[...], again_ref[...])
    projected_low = grad_projected.astype(BF)
    gatt_ref[...] = dot(proj_ref[...], projected_low, 1, 1).astype(BF)
    vectors_ref[0:1, :] = col_sum(grad_projected) * FACTOR
    vectors_ref[1:2, :] = col_sum(grad_middle * attn_normed) * FACTOR
    vectors_ref[2:3, :] = col_sum(grad_middle) * FACTOR
    grad_proj = dot(att_ref[...], projected_low, 1, 0) * FACTOR
    for c in range(4):
        gproj_ref[pl.ds(c, D, stride=4), :] = grad_proj[:, c * 128 : (c + 1) * 128]


def window_kernel(mixed_ref, gmiddle_ref, qkv_ref, own_ref, down_ref, right_ref, diag_ref):
    window = gmiddle_ref[...] + dot(mixed_ref[...], qkv_ref[...], 1, 1)
    window = window.astype(BF).reshape(WIN, WIN, D)
    own_ref[...] = window[:HALF, :HALF]
    right_ref[...] = window[:HALF, HALF:]
    down_ref[...] = window[HALF:, :HALF]
    diag_ref[...] = window[HALF:, HALF:]


def heads_kernel(
    probs_ref, qunit_ref, kunit_ref, inverse_ref, value_ref, gatt_s,
    logit_ref,
    mixed_ref, sums_ref, wide_s,
    qlow_s, klow_s, gmixed_s,
):
    qlow_s[...] = qunit_ref[...].astype(BF)
    klow_s[...] = kunit_ref[...].astype(BF)

    def head(h, carry):
        at = pl.ds(pl.multiple_of(h * E, E), E)
        kat = pl.ds(pl.multiple_of(h * E + D, E), E)
        vat = pl.ds(pl.multiple_of(h * E + 2 * D, E), E)
        scale = jnp.exp(jnp.minimum(jnp.full((1, T), logit_ref[h], F4), LOG_CAP))
        qlow, klow, gatt = qlow_s[at, :], klow_s[at, :], gatt_s[at, :]
        probs = probs_ref[h]
        grad_probs = dot(value_ref[at, :], gatt, 0, 0)
        gmixed_s[vat, :] = dot(gatt, probs.astype(BF), 1, 1)
        grad_scores = probs * (grad_probs - jnp.sum(probs * grad_probs, 0, keepdims=True))
        cosine = dot(klow, qlow, 0, 0)
        live = jnp.full((1, T), logit_ref[h], F4) < LOG_CAP
        total = jnp.sum(jnp.sum(grad_scores * cosine, 0, keepdims=True), 1, keepdims=True)
        term = jnp.where(live, total * scale * FACTOR, 0.0)
        lane = lax.broadcasted_iota(jnp.int32, (1, T), 1)
        carry = carry + jnp.where(lane == h, term, 0.0)
        grad_cosine = (grad_scores * scale).astype(BF)
        for index, (part, unit_ref, where) in enumerate(
            (
                (dot(klow, grad_cosine, 1, 0), qunit_ref, at),
                (dot(qlow, grad_cosine, 1, 1), kunit_ref, kat),
            )
        ):
            unit = unit_ref[at, :]
            gmixed_s[where, :] = inverse_ref[index, h] * (
                part - unit * jnp.sum(unit * part, 0, keepdims=True)
            )
        wide = None
        for p in range(8):
            first = grad_scores[(15 - p) * 16 : (16 - p) * 16]
            second = grad_scores[(7 - p) * 16 : (8 - p) * 16]
            blank = jnp.zeros((WIN, 128), F4)
            placed = jnp.concatenate(
                [first[:, :128], first[:, 128:] + second[:, :128], second[:, 128:], blank], 1
            )
            if p:
                placed = pltpu.roll(placed, 16 * p, 1)
            wide = placed if wide is None else wide + placed
        wide_s[h] = wide
        return carry

    logits = lax.fori_loop(0, HEADS, head, jnp.zeros((1, T), F4), unroll=4)
    sums_ref[2:3, :] = jnp.concatenate([logits, jnp.zeros((1, D - T), F4)], 1)

    ones = jnp.ones((8, T), F4)
    sums_ref[0:1, :] = few_by_wide(ones, gmixed_s[0:D, :], 1)[:1] * FACTOR
    sums_ref[1:2, :] = few_by_wide(ones, gmixed_s[2 * D :, :], 1)[:1] * FACTOR
    mixed_ref[...] = gmixed_s[...].astype(BF).T


def grads_kernel(x_ref, mixed_ref, gproj_ref, core_ref, keep_ref, send_ref, grads_s):
    mixed = mixed_ref[...]
    for c in range(4):
        cut = slice(c * 384, (c + 1) * 384)
        spread(grads_s, 0, c, dot(x_ref[...], mixed[:, cut], 1, 0) * FACTOR)
    grads = jnp.concatenate([grads_s[0], grads_s[1], grads_s[2], gproj_ref[...]], 1)
    split_cores(core_ref[0], ordered(grads, 0), ordered(grads, 1), keep_ref, send_ref, 0)


def table_kernel(
    entry_ref, mid_ref, exit_ref, squashed_ref, wide_s,
    sums_ref, attn_ref, mlp_ref, hsum_ref,
    small_ref,
    small_s,
):
    small_s[0:2, :] = sums_ref[0:2, :]
    small_s[2:5, :] = attn_ref[...]
    small_s[5:8, :] = mlp_ref[...]
    for c in range(0, FF, D):
        small_s[8 + c // D : 9 + c // D, :] = hsum_ref[:, c : c + D]
    small_s[31:32, :] = sums_ref[2:3, :]
    low = low_half((HEADS, LANES))
    even = jnp.zeros((HEADS, LANES), F4)
    odd = jnp.zeros((HEADS, LANES), F4)
    for c in range(WIN):
        part = wide_s[:, c, :]
        even += pltpu.roll(jnp.where(low, part, 0.0), (15 - c) % LANES, 1)
        odd += pltpu.roll(jnp.where(low, 0.0, part), (LANES - 1 - c) % LANES, 1)
    coords, valid = offset_coords()
    squashed = squashed_ref[...]
    table = jnp.concatenate([even, odd], 1) * 16.0 * squashed * (1.0 - squashed) * FACTOR
    table = jnp.where(valid[:1], table, 0.0)
    before = few_rows(stack_rows(entry_ref[...], mid_ref[...]), coords)
    small_s[15:31, :] = few_by_wide(table, jnp.maximum(before, 0.0), 1)
    grad_pos = jnp.where(before > 0.0, few_rows(exit_ref[...], table), 0.0)
    small_s[12:15, :] = few_by_wide(coords, grad_pos, 1)[:3]
    small = small_s[...]
    for c in range(4):
        small_ref[pl.ds(c, 32, stride=4), :] = small[:, c * 128 : (c + 1) * 128]


def shape(*dims, dtype=F4):
    return jax.ShapeDtypeStruct(dims, dtype)


def vmem(*dims, dtype=F4):
    return pltpu.VMEM(dims, dtype)


def whole(count, scalar=(), far=()):
    def space(i):
        return pltpu.SMEM if i in scalar else pl.ANY if i in far else pltpu.VMEM

    return [pl.BlockSpec(memory_space=space(i)) for i in range(count)]


def device_index(row, col):
    return (row % 16) * 16 + col % 16


def moved(block, rows, cols):
    route = [
        (device_index(r, c), device_index(r + rows, c + cols)) for r in range(16) for c in range(16)
    ]
    return lax.ppermute(block, ALL, route)


def swapped(block):
    return lax.ppermute(block, "core", [(0, 1), (1, 0)])


def joint(keep, got):
    return (keep.astype(F4) + got.astype(F4)).astype(BF)


def exchanged(blocks, axes):
    return lax.all_to_all(blocks, axes, 0, 0)


def rounds(small, steps):
    for axis, size, step in steps:
        small = small + lax.ppermute(small, axis, [(i, i ^ step) for i in range(size)])
    return small


def across(block):
    return lax.ppermute(block, "z", [(i, i ^ 1) for i in range(8)])


def cost(us):
    return pl.CostEstimate(flops=int(us * 5e8), bytes_accessed=int(us * 2e6), transcendentals=0)


def local(
    tokens, cotangent, regions, qkv_weight, query_bias, value_bias, logit_scale,
    entry_weight, entry_bias, exit_weight, proj_weight, proj_bias, attn_gain, attn_shift,
    hidden_weight, hidden_bias, output_weight, output_bias, mlp_gain,
):
    row = lambda v: v.reshape(1, -1)

    def strip(rows, cols):
        return jnp.concatenate([tokens[:, rows, cols], cotangent[:, rows, cols]], 0)

    head, tail = slice(0, HALF), slice(HALF, WIN)
    down = moved(strip(head, tail), -1, 0)
    right = moved(strip(tail, head), 0, -1)
    diag = moved(strip(head, head), -1, -1)
    exit_turned = exit_weight.T
    wide, squashed = pl.pallas_call(
        bias_kernel,
        out_shape=(
            shape(HEADS, WIN, LANES), shape(HEADS, 2 * LANES),
        ),
        in_specs=whole(3),
        out_specs=tuple(whole(2)),
        scratch_shapes=[vmem(WIN, HEADS, LANES)],
        compiler_params=PARAMS,
        cost_estimate=cost(5),
        name="bias",
    )(entry_weight, row(entry_bias), exit_turned)
    core = lax.axis_index("core").astype(jnp.int32).reshape(1)
    line = lax.axis_index("z").astype(jnp.int32).reshape(1)
    (
        x, probs, qunit, kunit, inverse, value, att, normed, ainverse, gmiddle,
        mlp_vectors, hidden_sum, keep, send,
    ) = pl.pallas_call(
        forward_kernel,
        out_shape=(
            shape(D, T, dtype=BF), shape(HEADS, T, T), shape(D, T), shape(D, T),
            shape(2, HEADS, 1, T), shape(D, T, dtype=BF), shape(D, T, dtype=BF),
            shape(T, D), shape(T, 1), shape(T, D), shape(3, D), shape(1, FF),
            shape(FF, D, dtype=BF), shape(FF, D, dtype=BF),
        ),
        in_specs=whole(22, (10, 20, 21), (15, 17)),
        out_specs=tuple(whole(14, (), (0, 1, 2, 3, 5, 6, 7, 9))),
        scratch_shapes=[
            vmem(D, T, dtype=BF), vmem(D, T, dtype=BF), vmem(T, FF, dtype=BF), vmem(T, FF),
            vmem(4, FF, 128), vmem(FF, D),
            vmem(D, FF, dtype=BF), vmem(FF, D, dtype=BF), vmem(D, T, dtype=BF),
            vmem(HEADS, T, T), vmem(D, T), vmem(D, T), vmem(D, T, dtype=BF),
            vmem(D, T, dtype=BF), vmem(T, D), vmem(T, D), pltpu.SemaphoreType.DMA((10,)),
        ],
        compiler_params=PARAMS,
        cost_estimate=cost(17),
        name="forward",
    )(
        tokens, cotangent, down, right, diag, regions, wide,
        qkv_weight, row(query_bias), row(value_bias), logit_scale,
        proj_weight, row(proj_bias), row(attn_gain), row(attn_shift),
        hidden_weight, row(hidden_bias), output_weight, row(output_bias), row(mlp_gain), core, line,
    )
    got = swapped(send)
    grad_att, grad_proj, attn_vectors = pl.pallas_call(
        middle_kernel,
        out_shape=(shape(D, T, dtype=BF), shape(FF, 128), shape(3, D)),
        in_specs=whole(6),
        out_specs=tuple(whole(3)),
        compiler_params=PARAMS,
        cost_estimate=cost(0.5),
        name="middle",
    )(att, normed, ainverse, gmiddle, proj_weight, row(attn_gain))
    early = jnp.concatenate(
        [
            joint(keep[:1024], got[:1024]).reshape(PLANE, 64, D),
            joint(keep[1024:DIRECT], got[1024:DIRECT]).reshape(PLANE, 32, D),
        ],
        1,
    )
    far = joint(keep[DIRECT + 256 :], got[DIRECT + 256 :])
    near = joint(keep[DIRECT : DIRECT + 256], got[DIRECT : DIRECT + 256])
    early, far, near, grad_att = lax.optimization_barrier((early, far, near, grad_att))
    far = across(far)
    early = exchanged(early, PLANE_AXES)
    mixed, token_sums, wide = pl.pallas_call(
        heads_kernel,
        out_shape=(shape(T, 3 * D, dtype=BF), shape(3, D), shape(HEADS, WIN, LANES)),
        in_specs=whole(7, (6,)),
        out_specs=tuple(whole(3)),
        scratch_shapes=[vmem(D, T, dtype=BF), vmem(D, T, dtype=BF), vmem(3 * D, T)],
        compiler_params=PARAMS,
        cost_estimate=cost(0.5),
        name="heads",
    )(probs, qunit, kunit, inverse, value, grad_att, logit_scale)
    small = pl.pallas_call(
        table_kernel,
        out_shape=shape(128, 128),
        in_specs=whole(9),
        out_specs=whole(1)[0],
        scratch_shapes=[vmem(32, D)],
        compiler_params=PARAMS,
        cost_estimate=cost(0.5),
        name="table",
    )(
        entry_weight, row(entry_bias), exit_turned, squashed, wide,
        token_sums, attn_vectors, mlp_vectors, hidden_sum,
    )
    mixed, far, small = lax.optimization_barrier((mixed, far, small))
    keep, send = pl.pallas_call(
        grads_kernel,
        out_shape=(shape(FF // 2, D, dtype=BF), shape(FF // 2, D, dtype=BF)),
        in_specs=whole(4, (3,)),
        out_specs=tuple(whole(2)),
        scratch_shapes=[vmem(3, FF, 128)],
        compiler_params=PARAMS,
        cost_estimate=cost(0.5),
        name="grads",
    )(x, mixed, grad_proj, core)
    got = swapped(send)
    small = small + swapped(small)
    mixed, small = lax.optimization_barrier((mixed, small))
    small = rounds(small, (("z", 8, 1),))
    back_own, back_down, back_right, back_diag = pl.pallas_call(
        window_kernel,
        out_shape=tuple(shape(HALF, HALF, D, dtype=BF) for _ in range(4)),
        in_specs=whole(3),
        out_specs=tuple(whole(4)),
        compiler_params=PARAMS,
        cost_estimate=cost(2),
        name="window",
    )(mixed, gmiddle, qkv_weight)
    got, keep, early, small, back_own, back_down, back_right, back_diag = lax.optimization_barrier(
        (got, keep, early, small, back_own, back_down, back_right, back_diag)
    )
    early = jnp.sum(early.astype(F4), 0)
    late = jnp.concatenate(
        [joint(keep, got).reshape(PLANE, 64, D), joint(near, far).reshape(PLANE, 16, D)], 1
    )
    late = exchanged(late, PLANE_AXES)
    small = rounds(small, (("z", 8, 2), ("z", 8, 4), ("x", 4, 1), ("x", 4, 2)))
    from_above = moved(back_down, 1, 0)
    from_left = moved(back_right, 0, 1)
    from_diag = moved(back_diag, 1, 1)
    grad_tokens = jnp.concatenate(
        [
            jnp.concatenate([from_diag, from_above], 1),
            jnp.concatenate([from_left, back_own], 1),
        ],
        0,
    )[None]
    late, small, grad_tokens = lax.optimization_barrier((late, small, grad_tokens))
    small = rounds(small, (("yl", 2, 1),))
    blocks = pl.pallas_call(
        line_kernel,
        out_shape=shape(8, 24, D, dtype=BF),
        in_specs=whole(3, (2,)),
        out_specs=whole(1)[0],
        compiler_params=PARAMS,
        cost_estimate=cost(2),
        name="line",
    )(early, late, line)
    blocks = exchanged(blocks, "z")
    others = lax.ppermute(small, "yh", [(0, 1), (1, 0)])
    (
        sum_hidden, sum_output, sum_qkv, sum_proj,
        vectors, hidden_total, logit_total, first, second,
    ) = pl.pallas_call(
        finish_kernel,
        out_shape=(
            shape(8 * D), shape(8 * D), shape(8 * 384), shape(8 * 128),
            shape(8, D), shape(FF), shape(HEADS), shape(3, D), shape(HEADS, D),
        ),
        in_specs=whole(3),
        out_specs=tuple(whole(9)),
        compiler_params=PARAMS,
        cost_estimate=cost(1),
        name="finish",
    )(blocks, small, others)
    return (
        grad_tokens,
        sum_qkv,
        sum_proj,
        sum_hidden,
        sum_output,
        vectors,
        hidden_total,
        logit_total,
        first,
        second.T,
    )


def solution(mesh):
    fine = Mesh(mesh.devices.reshape([n for _, n in AXES]), ALL)
    tile = P(None, ("z", "yh"), ("yl", "x", "core"))
    return jax.shard_map(
        local,
        mesh=fine,
        in_specs=(tile, tile, tile) + (P(),) * 16,
        out_specs=(tile,) + (P(ALL),) * 4 + (P(),) * 5,
        check_vma=False,
    )
```

```python
import math

import jax
import jax.numpy as jnp
from jax import lax
from jax.experimental import pallas as pl
from jax.experimental.pallas import tpu as pltpu
from jax.sharding import Mesh
from jax.sharding import PartitionSpec as P

WIN = 16
HALF = 8
T = 256
D = 512
HEADS = 16
E = 32
FF = 2048
CH = 512
LANES = 512
ALL = ("z", "yh", "yl", "x", "core")
AXES = (("z", 8), ("yh", 2), ("yl", 2), ("x", 4), ("core", 2))
PLANE = 16
DIRECT = 1536
PLANE_AXES = ALL[1:4]
FACTOR = 1.0 / 256.0
LOG_CAP = math.log(100.0)
TOP = lax.Precision.HIGHEST
BF = jnp.bfloat16
F4 = jnp.float32
PARAMS = pltpu.CompilerParams(vmem_limit_bytes=56 * 1024 * 1024)


def dot(a, b, ca, cb, precision=None):
    return lax.dot_general(
        a, b, (((ca,), (cb,)), ((), ())), precision=precision, preferred_element_type=F4
    )


def split(value, count):
    parts = []
    for _ in range(count):
        parts.append(value.astype(BF).astype(F4))
        value = value - parts[-1]
    return parts


def few_rows(a, b):
    a1, a2, a3 = split(a, 3)
    b1, b2, b3 = split(b, 3)
    left = jnp.concatenate([a1, a1, a2, a2, a1, a3], 0).astype(BF)
    right = jnp.concatenate([b1, b2, b1, b2, b3, b1], 0).astype(BF)
    return dot(left, right, 0, 0)


def few_by_wide(a, b, cb):
    rows = a.shape[0]
    left = jnp.concatenate(split(a, 2), 0).astype(BF)
    high, low = [part.astype(BF) for part in split(b, 2)]
    first, second = dot(left, high, 1, cb), dot(left, low, 1, cb)
    return first[:rows] + (first[rows:] + second[:rows])


def layer_stats(inputs):
    center = inputs - jnp.mean(inputs, -1, keepdims=True)
    inverse = lax.rsqrt(jnp.mean(center * center, -1, keepdims=True) + 1e-05)
    return center * inverse, inverse


def layer_back(upstream, normed, inverse, gain):
    scaled = upstream * gain
    inner = (
        scaled
        - jnp.mean(scaled, -1, keepdims=True)
        - normed * jnp.mean(scaled * normed, -1, keepdims=True)
    )
    return inverse * inner


def col_sum(block):
    return jnp.sum(block, 0, keepdims=True)


def offset_coords():
    lane = lax.broadcasted_iota(jnp.int32, (8, 2 * LANES), 1)
    parity = lane // LANES
    rest = lane - parity * LANES
    pair = rest // 32
    first = 2 * pair + parity
    second = rest - pair * 32
    valid = (first < 31) & (second < 31)

    def logged(index):
        u = (index.astype(F4) - 15.0) / 15.0 * 8.0
        size = jnp.log2(jnp.abs(u) + 1.0) / 3.0
        return jnp.where(u > 0.0, size, jnp.where(u < 0.0, -size, 0.0))

    row = lax.broadcasted_iota(jnp.int32, (8, 2 * LANES), 0)
    coords = jnp.where(
        row == 0, logged(first), jnp.where(row == 1, logged(second), jnp.where(row == 2, 1.0, 0.0))
    )
    return coords, valid


def low_half(shape):
    lane = lax.broadcasted_iota(jnp.int32, shape, len(shape) - 1)
    return lane % 32 < 16


def stack_rows(entry, bias):
    return jnp.concatenate([entry, bias, jnp.zeros((5, entry.shape[1]), F4)], 0)


def spread(ref, block, part, term):
    for lane in range(0, term.shape[1], 128):
        ref[block + lane // 128, pl.ds(part, D, stride=4), :] = term[:, lane : lane + 128]


def joined(ref):
    return jnp.concatenate([ref[b] for b in range(4)], 1)


def ordered(term, core):
    parts = term.reshape(8, PLANE, 2, 8, term.shape[1])
    cut = [parts[:, i, core] for i in range(PLANE)]
    return jnp.concatenate(cut, 0).reshape(-1, term.shape[1])


def paired(term, core):
    parts = term.reshape(8, PLANE, 2, 8, term.shape[1])
    cut = [jnp.concatenate([parts[:4, i, core], parts[4:, i, core]], 2) for i in range(PLANE)]
    return jnp.concatenate(cut, 0).reshape(-1, 2 * term.shape[1])


def paired_lines(term, core, lines):
    parts = term.reshape(4, 2, PLANE, 2, 8, term.shape[1])[:, lines]
    cut = [jnp.concatenate([parts[:2, i, core], parts[2:, i, core]], 2) for i in range(PLANE)]
    return jnp.concatenate(cut, 0).reshape(-1, 2 * term.shape[1])


def split_cores(core, first, second, keep_ref, send_ref, start):
    rows = pl.ds(start, first.shape[0])
    keep_ref[rows, :] = jnp.where(core == 0, first, second).astype(BF)
    send_ref[rows, :] = jnp.where(core == 0, second, first).astype(BF)


def line_kernel(early_ref, late_ref, line_ref, out_ref):
    early = early_ref[...]
    late = jnp.sum(late_ref[...].astype(F4), 0)
    half = D // 2
    for z in range(8):
        rows = slice(8 * z, 8 * z + 8)
        spot = 64 + 8 * (z % 4)
        direct = early[spot : spot + 8, z // 4 * half : (z // 4 + 1) * half]
        spot = 64 + 8 * (z // 2 % 2)
        turned = late[spot : spot + 8, z // 4 * half : (z // 4 + 1) * half]
        turned = jnp.where(line_ref[0] % 2 == z % 2, turned, 0.0)
        output = jnp.concatenate([direct, turned], 1)
        out_ref[z] = jnp.concatenate([early[rows], output, late[rows]], 0).astype(BF)


def finish_kernel(
    blocks_ref, small_ref, others_ref,
    hidden_ref, output_ref, qkv_ref, proj_ref,
    vectors_ref, hbias_ref, logit_ref, first_ref, second_ref,
):
    total = jnp.sum(blocks_ref[...].astype(F4), 0)
    for r in range(8):
        hidden_ref[r * D : (r + 1) * D] = total[r]
        output_ref[r * D : (r + 1) * D] = total[8 + r]
        qkv_ref[r * 384 : (r + 1) * 384] = total[16 + r, :384]
        proj_ref[r * 128 : (r + 1) * 128] = total[16 + r, 384:]
    rows = [pl.ds(c, 32, stride=4) for c in range(4)]
    total = jnp.concatenate([small_ref[r, :] + others_ref[r, :] for r in rows], 1)
    vectors_ref[...] = total[:8]
    for c in range(4):
        hbias_ref[c * D : (c + 1) * D] = total[8 + c]
    first_ref[...] = total[12:15]
    second_ref[...] = total[15:31]
    logit_ref[...] = total[31, :HEADS]


def bias_kernel(entry_ref, mid_ref, exit_ref, wide_ref, squashed_ref, scratch):
    coords, _ = offset_coords()
    before = few_rows(stack_rows(entry_ref[...], mid_ref[...]), coords)
    hidden = jnp.maximum(before, 0.0)
    squashed = jax.nn.sigmoid(few_by_wide(exit_ref[...], hidden, 0))
    squashed_ref[...] = squashed
    table = 16.0 * squashed
    even, odd = table[:, :LANES], table[:, LANES:]
    low = low_half((HEADS, LANES))
    for c in range(WIN):
        scratch[c] = jnp.where(
            low,
            pltpu.roll(even, (c - 15) % LANES, 1),
            pltpu.roll(odd, (c + 1) % LANES, 1),
        )
    for h in range(HEADS):
        wide_ref[h] = scratch[:, h, :]


def forward_kernel(
    tokens_ref, cotangent_ref, down_ref, right_ref, diag_ref, regions_ref, wide_ref,
    qkv_ref, qbias_ref, vbias_ref, logit_ref,
    proj_ref, pbias_ref, again_ref, ashift_ref,
    hidden_ref, hbias_ref, output_ref, obias_ref, mgain_ref, core_ref, line_ref,
    x_ref, probs_ref, qunit_ref, kunit_ref, inverse_ref, value_ref, att_ref,
    normed_ref, ainverse_ref, gmiddle_ref, vectors_ref, hsum_ref, keep_ref, send_ref,
    qlow_s, klow_s, act_s, slope_s, ghidden_s, goutput_s,
    whidden_s, woutput_s, x_s, probs_s, qunit_s, kunit_s, value_s, att_s, normed_s, gmiddle_s, sems,
):
    loads = [
        pltpu.make_async_copy(hidden_ref, whidden_s, sems.at[0]),
        pltpu.make_async_copy(output_ref, woutput_s, sems.at[1]),
    ]
    for load in loads:
        load.start()
    stores = []

    def store(scratch, ref):
        stores.append(pltpu.make_async_copy(scratch, ref, sems.at[2 + len(stores)]))
        stores[-1].start()

    def assemble(own_ref, i):
        top = jnp.concatenate([own_ref[0, HALF:, HALF:], right_ref[i]], 1)
        bottom = jnp.concatenate([down_ref[i], diag_ref[i]], 1)
        return jnp.concatenate([top, bottom], 0).reshape(T, D)

    x = assemble(tokens_ref, 0)
    x_s[...] = x.T
    store(x_s, x_ref)
    mixed = dot(x, qkv_ref[...], 1, 0)
    q = (mixed[:, :D] + qbias_ref[...]).T
    k = mixed[:, D : 2 * D].T
    value_s[...] = (mixed[:, 2 * D :] + vbias_ref[...]).T.astype(BF)
    for index, (raw, unit_ref, low_s) in enumerate(
        ((q, qunit_s, qlow_s), (k, kunit_s, klow_s))
    ):
        split = raw.reshape(HEADS, E, T)
        inverse = lax.rsqrt(jnp.sum(split * split, 1, keepdims=True) + 1e-06)
        inverse_ref[index] = inverse
        unit = (split * inverse).reshape(D, T)
        unit_ref[...] = unit
        low_s[...] = unit.astype(BF)
    store(qunit_s, qunit_ref)
    store(kunit_s, kunit_ref)
    store(value_s, value_ref)
    own_row = lax.broadcasted_iota(jnp.int32, (WIN, T), 0)
    token = lax.broadcasted_iota(jnp.int32, (WIN, T), 1)
    pick = jnp.where(token % WIN == own_row, 1.0, 0.0).astype(BF)
    by_row = dot(regions_ref[0].astype(F4).astype(BF), pick, 1, 0)
    region_row = col_sum(jnp.where(token // WIN == own_row, by_row, 0.0))
    region_col = jnp.broadcast_to(region_row, (8, T)).T[:, :1]
    allowed = region_col == region_row

    def head(h, carry):
        at = pl.ds(pl.multiple_of(h * E, E), E)
        scale = jnp.exp(jnp.minimum(jnp.full((1, T), logit_ref[h], F4), LOG_CAP))
        cosine = dot(klow_s[at, :], qlow_s[at, :], 0, 0)
        wide = wide_ref[h]
        rolled = [wide] + [pltpu.roll(wide, LANES - 16 * p, 1) for p in range(1, 8)]
        bias = jnp.concatenate(
            [
                rolled[(15 - r) % 8][:, (15 - r) // 8 * 128 : (15 - r) // 8 * 128 + T]
                for r in range(WIN)
            ],
            0,
        )
        logits = jnp.where(allowed, scale * cosine + bias, -1000000000.0)
        powers = jnp.exp(logits - jnp.max(logits, 0, keepdims=True))
        probs = powers * (1.0 / jnp.sum(powers, 0, keepdims=True))
        probs_s[h] = probs
        pltpu.make_async_copy(probs_s.at[h], probs_ref.at[h], sems.at[9]).start()
        att_s[at, :] = dot(value_s[at, :], probs.astype(BF), 1, 0).astype(BF)
        return carry

    lax.fori_loop(0, HEADS, head, 0, unroll=8)

    store(att_s, att_ref)
    projected = dot(att_s[...], proj_ref[...], 0, 0) + pbias_ref[...]
    attn_normed, attn_inverse = layer_stats(projected)
    normed_s[...] = attn_normed
    store(normed_s, normed_ref)
    ainverse_ref[...] = attn_inverse
    middle = x.astype(F4) + (attn_normed * again_ref[...] + ashift_ref[...])
    middle_low = middle.astype(BF)
    for load in loads:
        load.wait()
    emitted = jnp.zeros((T, D), F4)
    for c in range(0, FF, CH):
        cut = slice(c, c + CH)
        before = dot(middle_low, whidden_s[:, cut], 1, 0) + hbias_ref[:, cut]
        cumulative = 0.5 * (1.0 + lax.erf(before * (1.0 / math.sqrt(2.0))))
        density = jnp.exp(-0.5 * before * before) * (1.0 / math.sqrt(2.0 * math.pi))
        slope_s[:, cut] = cumulative + before * density
        act = (before * cumulative).astype(BF)
        act_s[:, cut] = act
        emitted += dot(act, woutput_s[cut, :], 1, 0)
    normed, inverse = layer_stats(emitted + obias_ref[...])
    incoming = assemble(cotangent_ref, 1).astype(F4)
    grad_emitted = layer_back(incoming, normed, inverse, mgain_ref[...])
    emitted_low = grad_emitted.astype(BF)
    vectors_ref[0:1, :] = col_sum(grad_emitted) * FACTOR
    vectors_ref[1:2, :] = col_sum(incoming * normed) * FACTOR
    vectors_ref[2:3, :] = col_sum(incoming) * FACTOR
    grad_middle = incoming
    for c in range(0, FF, CH):
        cut = slice(c, c + CH)
        grad_act = dot(emitted_low, woutput_s[cut, :], 1, 1)
        grad_before = grad_act * slope_s[:, cut]
        hsum_ref[:, cut] = col_sum(grad_before) * FACTOR
        before_low = grad_before.astype(BF)
        goutput_s[cut, :] = dot(act_s[:, cut], emitted_low, 0, 0) * FACTOR
        spread(ghidden_s, 0, c // CH, dot(middle_low, before_low, 0, 0) * FACTOR)
        grad_middle += dot(before_low, whidden_s[:, cut], 1, 1)
    gmiddle_s[...] = grad_middle
    store(gmiddle_s, gmiddle_ref)
    core = core_ref[0]
    term = joined(ghidden_s)
    split_cores(core, ordered(term, 0), ordered(term, 1), keep_ref, send_ref, 0)
    term = goutput_s[...]
    even = line_ref[0] % 2 == 0
    half = D // 2
    direct, turned = term[:, :half], term[:, half:]
    split_cores(core, paired(direct, 0), paired(direct, 1), keep_ref, send_ref, FF // 2)
    halves = [[paired_lines(turned, k, lines) for lines in range(2)] for k in range(2)]
    near = [jnp.where(even, a, b) for a, b in halves]
    far = [jnp.where(even, b, a) for a, b in halves]
    split_cores(core, *near, keep_ref, send_ref, DIRECT)
    split_cores(core, *far, keep_ref, send_ref, DIRECT + 256)
    pltpu.make_async_copy(probs_s, probs_ref, sems.at[9]).wait()
    for done in stores:
        done.wait()


def middle_kernel(
    att_ref, normed_ref, ainverse_ref, gmiddle_ref, proj_ref, again_ref,
    gatt_ref, gproj_ref, vectors_ref,
):
    grad_middle = gmiddle_ref[...]
    attn_normed = normed_ref[...]
    grad_projected = layer_back(grad_middle, attn_normed, ainverse_ref[...], again_ref[...])
    projected_low = grad_projected.astype(BF)
    gatt_ref[...] = dot(proj_ref[...], projected_low, 1, 1).astype(BF)
    vectors_ref[0:1, :] = col_sum(grad_projected) * FACTOR
    vectors_ref[1:2, :] = col_sum(grad_middle * attn_normed) * FACTOR
    vectors_ref[2:3, :] = col_sum(grad_middle) * FACTOR
    grad_proj = dot(att_ref[...], projected_low, 1, 0) * FACTOR
    for c in range(4):
        gproj_ref[pl.ds(c, D, stride=4), :] = grad_proj[:, c * 128 : (c + 1) * 128]


def window_kernel(mixed_ref, gmiddle_ref, qkv_ref, own_ref, down_ref, right_ref, diag_ref):
    window = gmiddle_ref[...] + dot(mixed_ref[...], qkv_ref[...], 1, 1)
    window = window.astype(BF).reshape(WIN, WIN, D)
    own_ref[...] = window[:HALF, :HALF]
    right_ref[...] = window[:HALF, HALF:]
    down_ref[...] = window[HALF:, :HALF]
    diag_ref[...] = window[HALF:, HALF:]


def heads_kernel(
    probs_ref, qunit_ref, kunit_ref, inverse_ref, value_ref, gatt_s,
    logit_ref,
    mixed_ref, sums_ref, wide_s,
    qlow_s, klow_s, gmixed_s,
):
    qlow_s[...] = qunit_ref[...].astype(BF)
    klow_s[...] = kunit_ref[...].astype(BF)

    def head(h, carry):
        at = pl.ds(pl.multiple_of(h * E, E), E)
        kat = pl.ds(pl.multiple_of(h * E + D, E), E)
        vat = pl.ds(pl.multiple_of(h * E + 2 * D, E), E)
        scale = jnp.exp(jnp.minimum(jnp.full((1, T), logit_ref[h], F4), LOG_CAP))
        qlow, klow, gatt = qlow_s[at, :], klow_s[at, :], gatt_s[at, :]
        probs = probs_ref[h]
        grad_probs = dot(value_ref[at, :], gatt, 0, 0)
        gmixed_s[vat, :] = dot(gatt, probs.astype(BF), 1, 1)
        grad_scores = probs * (grad_probs - jnp.sum(probs * grad_probs, 0, keepdims=True))
        cosine = dot(klow, qlow, 0, 0)
        live = jnp.full((1, T), logit_ref[h], F4) < LOG_CAP
        total = jnp.sum(jnp.sum(grad_scores * cosine, 0, keepdims=True), 1, keepdims=True)
        term = jnp.where(live, total * scale * FACTOR, 0.0)
        lane = lax.broadcasted_iota(jnp.int32, (1, T), 1)
        carry = carry + jnp.where(lane == h, term, 0.0)
        grad_cosine = (grad_scores * scale).astype(BF)
        for index, (part, unit_ref, where) in enumerate(
            (
                (dot(klow, grad_cosine, 1, 0), qunit_ref, at),
                (dot(qlow, grad_cosine, 1, 1), kunit_ref, kat),
            )
        ):
            unit = unit_ref[at, :]
            gmixed_s[where, :] = inverse_ref[index, h] * (
                part - unit * jnp.sum(unit * part, 0, keepdims=True)
            )
        wide = None
        for p in range(8):
            first = grad_scores[(15 - p) * 16 : (16 - p) * 16]
            second = grad_scores[(7 - p) * 16 : (8 - p) * 16]
            blank = jnp.zeros((WIN, 128), F4)
            placed = jnp.concatenate(
                [first[:, :128], first[:, 128:] + second[:, :128], second[:, 128:], blank], 1
            )
            if p:
                placed = pltpu.roll(placed, 16 * p, 1)
            wide = placed if wide is None else wide + placed
        wide_s[h] = wide
        return carry

    logits = lax.fori_loop(0, HEADS, head, jnp.zeros((1, T), F4), unroll=8)
    sums_ref[2:3, :] = jnp.concatenate([logits, jnp.zeros((1, D - T), F4)], 1)

    ones = jnp.ones((8, T), F4)
    sums_ref[0:1, :] = few_by_wide(ones, gmixed_s[0:D, :], 1)[:1] * FACTOR
    sums_ref[1:2, :] = few_by_wide(ones, gmixed_s[2 * D :, :], 1)[:1] * FACTOR
    mixed_ref[...] = gmixed_s[...].astype(BF).T


def grads_kernel(x_ref, mixed_ref, gproj_ref, core_ref, keep_ref, send_ref, grads_s):
    mixed = mixed_ref[...]
    for c in range(4):
        cut = slice(c * 384, (c + 1) * 384)
        spread(grads_s, 0, c, dot(x_ref[...], mixed[:, cut], 1, 0) * FACTOR)
    grads = jnp.concatenate([grads_s[0], grads_s[1], grads_s[2], gproj_ref[...]], 1)
    split_cores(core_ref[0], ordered(grads, 0), ordered(grads, 1), keep_ref, send_ref, 0)


def table_kernel(
    entry_ref, mid_ref, exit_ref, squashed_ref, wide_s,
    sums_ref, attn_ref, mlp_ref, hsum_ref,
    small_ref,
    small_s,
):
    small_s[0:2, :] = sums_ref[0:2, :]
    small_s[2:5, :] = attn_ref[...]
    small_s[5:8, :] = mlp_ref[...]
    for c in range(0, FF, D):
        small_s[8 + c // D : 9 + c // D, :] = hsum_ref[:, c : c + D]
    small_s[31:32, :] = sums_ref[2:3, :]
    low = low_half((HEADS, LANES))
    even = jnp.zeros((HEADS, LANES), F4)
    odd = jnp.zeros((HEADS, LANES), F4)
    for c in range(WIN):
        part = wide_s[:, c, :]
        even += pltpu.roll(jnp.where(low, part, 0.0), (15 - c) % LANES, 1)
        odd += pltpu.roll(jnp.where(low, 0.0, part), (LANES - 1 - c) % LANES, 1)
    coords, valid = offset_coords()
    squashed = squashed_ref[...]
    table = jnp.concatenate([even, odd], 1) * 16.0 * squashed * (1.0 - squashed) * FACTOR
    table = jnp.where(valid[:1], table, 0.0)
    before = few_rows(stack_rows(entry_ref[...], mid_ref[...]), coords)
    small_s[15:31, :] = few_by_wide(table, jnp.maximum(before, 0.0), 1)
    grad_pos = jnp.where(before > 0.0, few_rows(exit_ref[...], table), 0.0)
    small_s[12:15, :] = few_by_wide(coords, grad_pos, 1)[:3]
    small = small_s[...]
    for c in range(4):
        small_ref[pl.ds(c, 32, stride=4), :] = small[:, c * 128 : (c + 1) * 128]


def shape(*dims, dtype=F4):
    return jax.ShapeDtypeStruct(dims, dtype)


def vmem(*dims, dtype=F4):
    return pltpu.VMEM(dims, dtype)


def whole(count, scalar=(), far=()):
    def space(i):
        return pltpu.SMEM if i in scalar else pl.ANY if i in far else pltpu.VMEM

    return [pl.BlockSpec(memory_space=space(i)) for i in range(count)]


def device_index(row, col):
    return (row % 16) * 16 + col % 16


def moved(block, rows, cols):
    route = [
        (device_index(r, c), device_index(r + rows, c + cols)) for r in range(16) for c in range(16)
    ]
    return lax.ppermute(block, ALL, route)


def swapped(block):
    return lax.ppermute(block, "core", [(0, 1), (1, 0)])


def joint(keep, got):
    return (keep.astype(F4) + got.astype(F4)).astype(BF)


def exchanged(blocks, axes):
    return lax.all_to_all(blocks, axes, 0, 0)


def rounds(small, steps):
    for axis, size, step in steps:
        small = small + lax.ppermute(small, axis, [(i, i ^ step) for i in range(size)])
    return small


def across(block):
    return lax.ppermute(block, "z", [(i, i ^ 1) for i in range(8)])


def cost(us):
    return pl.CostEstimate(flops=int(us * 5e8), bytes_accessed=int(us * 2e6), transcendentals=0)


def local(
    tokens, cotangent, regions, qkv_weight, query_bias, value_bias, logit_scale,
    entry_weight, entry_bias, exit_weight, proj_weight, proj_bias, attn_gain, attn_shift,
    hidden_weight, hidden_bias, output_weight, output_bias, mlp_gain,
):
    row = lambda v: v.reshape(1, -1)

    def strip(rows, cols):
        return jnp.concatenate([tokens[:, rows, cols], cotangent[:, rows, cols]], 0)

    head, tail = slice(0, HALF), slice(HALF, WIN)
    down = moved(strip(head, tail), -1, 0)
    right = moved(strip(tail, head), 0, -1)
    diag = moved(strip(head, head), -1, -1)
    exit_turned = exit_weight.T
    wide, squashed = pl.pallas_call(
        bias_kernel,
        out_shape=(
            shape(HEADS, WIN, LANES), shape(HEADS, 2 * LANES),
        ),
        in_specs=whole(3),
        out_specs=tuple(whole(2)),
        scratch_shapes=[vmem(WIN, HEADS, LANES)],
        compiler_params=PARAMS,
        cost_estimate=cost(5),
        name="bias",
    )(entry_weight, row(entry_bias), exit_turned)
    core = lax.axis_index("core").astype(jnp.int32).reshape(1)
    line = lax.axis_index("z").astype(jnp.int32).reshape(1)
    (
        x, probs, qunit, kunit, inverse, value, att, normed, ainverse, gmiddle,
        mlp_vectors, hidden_sum, keep, send,
    ) = pl.pallas_call(
        forward_kernel,
        out_shape=(
            shape(D, T, dtype=BF), shape(HEADS, T, T), shape(D, T), shape(D, T),
            shape(2, HEADS, 1, T), shape(D, T, dtype=BF), shape(D, T, dtype=BF),
            shape(T, D), shape(T, 1), shape(T, D), shape(3, D), shape(1, FF),
            shape(FF, D, dtype=BF), shape(FF, D, dtype=BF),
        ),
        in_specs=whole(22, (10, 20, 21), (15, 17)),
        out_specs=tuple(whole(14, (), (0, 1, 2, 3, 5, 6, 7, 9))),
        scratch_shapes=[
            vmem(D, T, dtype=BF), vmem(D, T, dtype=BF), vmem(T, FF, dtype=BF), vmem(T, FF),
            vmem(4, FF, 128), vmem(FF, D),
            vmem(D, FF, dtype=BF), vmem(FF, D, dtype=BF), vmem(D, T, dtype=BF),
            vmem(HEADS, T, T), vmem(D, T), vmem(D, T), vmem(D, T, dtype=BF),
            vmem(D, T, dtype=BF), vmem(T, D), vmem(T, D), pltpu.SemaphoreType.DMA((10,)),
        ],
        compiler_params=PARAMS,
        cost_estimate=cost(17),
        name="forward",
    )(
        tokens, cotangent, down, right, diag, regions, wide,
        qkv_weight, row(query_bias), row(value_bias), logit_scale,
        proj_weight, row(proj_bias), row(attn_gain), row(attn_shift),
        hidden_weight, row(hidden_bias), output_weight, row(output_bias), row(mlp_gain), core, line,
    )
    got = swapped(send)
    grad_att, grad_proj, attn_vectors = pl.pallas_call(
        middle_kernel,
        out_shape=(shape(D, T, dtype=BF), shape(FF, 128), shape(3, D)),
        in_specs=whole(6),
        out_specs=tuple(whole(3)),
        compiler_params=PARAMS,
        cost_estimate=cost(0.5),
        name="middle",
    )(att, normed, ainverse, gmiddle, proj_weight, row(attn_gain))
    early = jnp.concatenate(
        [
            joint(keep[:1024], got[:1024]).reshape(PLANE, 64, D),
            joint(keep[1024:DIRECT], got[1024:DIRECT]).reshape(PLANE, 32, D),
        ],
        1,
    )
    far = joint(keep[DIRECT + 256 :], got[DIRECT + 256 :])
    near = joint(keep[DIRECT : DIRECT + 256], got[DIRECT : DIRECT + 256])
    early, far, near, grad_att = lax.optimization_barrier((early, far, near, grad_att))
    far = across(far)
    early = exchanged(early, PLANE_AXES)
    mixed, token_sums, wide = pl.pallas_call(
        heads_kernel,
        out_shape=(shape(T, 3 * D, dtype=BF), shape(3, D), shape(HEADS, WIN, LANES)),
        in_specs=whole(7, (6,)),
        out_specs=tuple(whole(3)),
        scratch_shapes=[vmem(D, T, dtype=BF), vmem(D, T, dtype=BF), vmem(3 * D, T)],
        compiler_params=PARAMS,
        cost_estimate=cost(0.5),
        name="heads",
    )(probs, qunit, kunit, inverse, value, grad_att, logit_scale)
    small = pl.pallas_call(
        table_kernel,
        out_shape=shape(128, 128),
        in_specs=whole(9),
        out_specs=whole(1)[0],
        scratch_shapes=[vmem(32, D)],
        compiler_params=PARAMS,
        cost_estimate=cost(0.5),
        name="table",
    )(
        entry_weight, row(entry_bias), exit_turned, squashed, wide,
        token_sums, attn_vectors, mlp_vectors, hidden_sum,
    )
    mixed, far, small = lax.optimization_barrier((mixed, far, small))
    keep, send = pl.pallas_call(
        grads_kernel,
        out_shape=(shape(FF // 2, D, dtype=BF), shape(FF // 2, D, dtype=BF)),
        in_specs=whole(4, (3,)),
        out_specs=tuple(whole(2)),
        scratch_shapes=[vmem(3, FF, 128)],
        compiler_params=PARAMS,
        cost_estimate=cost(0.5),
        name="grads",
    )(x, mixed, grad_proj, core)
    got = swapped(send)
    small = small + swapped(small)
    mixed, small = lax.optimization_barrier((mixed, small))
    small = rounds(small, (("z", 8, 1),))
    back_own, back_down, back_right, back_diag = pl.pallas_call(
        window_kernel,
        out_shape=tuple(shape(HALF, HALF, D, dtype=BF) for _ in range(4)),
        in_specs=whole(3),
        out_specs=tuple(whole(4)),
        compiler_params=PARAMS,
        cost_estimate=cost(2),
        name="window",
    )(mixed, gmiddle, qkv_weight)
    got, keep, early, small, back_own, back_down, back_right, back_diag = lax.optimization_barrier(
        (got, keep, early, small, back_own, back_down, back_right, back_diag)
    )
    early = jnp.sum(early.astype(F4), 0)
    late = jnp.concatenate(
        [joint(keep, got).reshape(PLANE, 64, D), joint(near, far).reshape(PLANE, 16, D)], 1
    )
    late = exchanged(late, PLANE_AXES)
    small = rounds(small, (("z", 8, 2), ("z", 8, 4), ("x", 4, 1), ("x", 4, 2)))
    from_above = moved(back_down, 1, 0)
    from_left = moved(back_right, 0, 1)
    from_diag = moved(back_diag, 1, 1)
    grad_tokens = jnp.concatenate(
        [
            jnp.concatenate([from_diag, from_above], 1),
            jnp.concatenate([from_left, back_own], 1),
        ],
        0,
    )[None]
    late, small, grad_tokens = lax.optimization_barrier((late, small, grad_tokens))
    small = rounds(small, (("yl", 2, 1),))
    blocks = pl.pallas_call(
        line_kernel,
        out_shape=shape(8, 24, D, dtype=BF),
        in_specs=whole(3, (2,)),
        out_specs=whole(1)[0],
        compiler_params=PARAMS,
        cost_estimate=cost(2),
        name="line",
    )(early, late, line)
    blocks = exchanged(blocks, "z")
    others = lax.ppermute(small, "yh", [(0, 1), (1, 0)])
    (
        sum_hidden, sum_output, sum_qkv, sum_proj,
        vectors, hidden_total, logit_total, first, second,
    ) = pl.pallas_call(
        finish_kernel,
        out_shape=(
            shape(8 * D), shape(8 * D), shape(8 * 384), shape(8 * 128),
            shape(8, D), shape(FF), shape(HEADS), shape(3, D), shape(HEADS, D),
        ),
        in_specs=whole(3),
        out_specs=tuple(whole(9)),
        compiler_params=PARAMS,
        cost_estimate=cost(1),
        name="finish",
    )(blocks, small, others)
    return (
        grad_tokens,
        sum_qkv,
        sum_proj,
        sum_hidden,
        sum_output,
        vectors,
        hidden_total,
        logit_total,
        first,
        second.T,
    )


def solution(mesh):
    fine = Mesh(mesh.devices.reshape([n for _, n in AXES]), ALL)
    tile = P(None, ("z", "yh"), ("yl", "x", "core"))
    return jax.shard_map(
        local,
        mesh=fine,
        in_specs=(tile, tile, tile) + (P(),) * 16,
        out_specs=(tile,) + (P(ALL),) * 4 + (P(),) * 5,
        check_vma=False,
    )
```
